256 devices in a mesh: dp: 16 (over y, x), leaf: 16 (over z, core).
Axes of the slice: x: 4, y: 4, z: 8, core: 2. Of those that a mesh axis runs over, the one named last changes fastest.
Arguments:
- audio_feats: bfloat16 [49152, 27, 512], P(('dp', 'leaf')), may hold values from -24 to 24
- conv_weight: bfloat16 [2, 3, 512, 512], replicated, may hold values from -0.15625 to 0.15625
- head_weight: bfloat16 [32768, 512], P('leaf'), may hold values from -0.25 to 0.25
- clip_owner: int32 [49152, 2], P(('dp', 'leaf')), may hold values from 0 to 15, all different within a row; in each aligned block of 192 rows (0 to 191, 192 to 383, ...) at most 48 rows name the same one
- node_ids: int32 [49152, 2, 8], P(('dp', 'leaf')), may hold values from 0 to 2047
Outputs:
- conv_grad: bfloat16 [2, 3, 512, 512], P(None, None, 'dp', 'leaf')
- head_grad: bfloat16 [32768, 512], P(('leaf', 'dp'))
The draws below stay inside these ranges and needn't reach their ends.
Inputs may be any that keep to these rules, and one draw needn't show every extreme that they name: `clip_owner`: each clip names 2 different owners; among the 192 clips of one device (aligned blocks of rows) no owner is named more than 48 times. `node_ids`: node indices are local to the owner named by the same route.
All inputs are finite; a program needn't handle non-finite values.
Results may differ from the reference program's by a relative error of at most 0.011.
Values may be sent and summed in bfloat16 or wider, within the bound.
A program may use at most 128 MiB of HBM per device.

```python
import math
import jax
import jax.numpy as jnp
import numpy as np
from jax import lax

C = 512
LAYERS = 2
L0 = 27
CL_DEV = 192
TOP = 2
NPAIR = 8
NPOS = 4
NODE_OWN = 2048
CAP = 48
CLIPS = 49152
NODES = 32768
N_LEAF = 16


def set_ends(drawn, key, low, high):
    extent = drawn.shape
    spot = [jax.random.randint(jax.random.fold_in(key, axis), (), 0, extent[axis]) for axis in range(len(extent))]
    drawn = drawn.at[tuple(spot)].set(low)
    longest = extent.index(max(extent))
    spot[longest] = (spot[longest] + 1) % extent[longest]
    return drawn.at[tuple(spot)].set(high)


def raised(entries, stream_key, source, target, parts, factor):
    owner, partner = [(jnp.arange(entries.shape[axis_at]) // (entries.shape[axis_at] // parts)).reshape([-1 if axis == axis_at else 1 for axis in range(entries.ndim)]) for axis_at in (source, target)]
    chosen = jax.random.permutation(stream_key, parts)[partner]
    strong = (owner == chosen) | (owner == (partner + parts // 2) % parts)
    return jnp.where(strong, factor * entries, entries)


def level_of(stream_key, shape, split, low, top_value):
    loudness = 1.0
    for position, shards_of in split:
        heights = jax.random.uniform(jax.random.fold_in(jax.random.fold_in(stream_key, 6), position), (shards_of,), jnp.float32, low / len(split), top_value / len(split))
        loudness = loudness * jnp.repeat(jnp.exp(heights), shape[position] // shards_of).reshape((-1,) + (1,) * (len(shape) - 1 - position))
    return loudness


def deal_out(own_key, own, number, rows, count, top, limit, slope):
    order = jax.random.permutation(own_key, count)
    packed, ordinary = load_shares(count, rows * top, limit, slope, True), load_shares(count, rows * top, limit, slope, False)
    places = jnp.arange(count)

    def named(tallies, turn):
        used = int((tallies > 0).sum())
        fixed = max(1, used // 4)
        moved = fixed + (places - fixed + turn * (used - fixed)) % max(1, count - fixed)
        return jnp.zeros((count,), jnp.int32).at[order[jnp.where(places < fixed, places, moved)]].set(jnp.asarray(tallies, jnp.int32))

    tallies = jnp.where(number % 4 == 0, named(packed, number // 4), named(ordinary, number - number // 4 - 1))
    mixed = jax.random.permutation(jax.random.fold_in(own, 3), count)
    donor, receiver = mixed[0:count // 2 * 2:2], mixed[1:count // 2 * 2:2]
    margin = jnp.minimum(tallies[donor] - 1, limit - tallies[receiver]) // 2
    margin = jnp.where((donor == order[0]) | (receiver == order[0]) | (tallies[receiver] == 0), 0, jnp.maximum(margin, 0))
    moved = jax.random.randint(jax.random.fold_in(own, 4), (count // 2,), 0, 1 << 20) % (margin + 1)
    tallies = tallies.at[donor].add(-moved).at[receiver].add(moved)
    items = jnp.searchsorted(jnp.cumsum(tallies), jnp.arange(rows * top), side="right").astype(jnp.int32)
    listing = items.reshape(top, rows).T
    listing = listing[jax.random.permutation(jax.random.fold_in(own, 1), rows)]
    turn = jax.random.randint(jax.random.fold_in(own, 2), (rows, 1), 0, top)
    return jnp.take_along_axis(listing, (jnp.arange(top)[None, :] + turn) % top, axis=1)


def load_shares(count, total, reach, slope, full):
    loads = [(1 << 20) // math.isqrt(grade ** slope) + 1 for grade in range(1, count + 1)]
    largest = reach if full else min(reach, max(-(-total // count), total * loads[0] // sum(loads)))
    least = 1 if total - largest >= count - 1 else 0
    counts, rest = [largest] + [least] * (count - 1), total - largest - least * (count - 1)
    while rest > 0:
        free = [i for i in range(1, count) if counts[i] < largest] or [i for i in range(1, count) if counts[i] < reach]
        pool, budget = sum([loads[i] for i in free]), rest
        for i in free:
            extra = min(reach - counts[i], max(1, budget * loads[i] // pool), rest)
            counts[i] = counts[i] + extra
            rest = rest - extra
    return np.array(counts)


def gaussian(key, dims, spread, limit, split=(), held_as=jnp.bfloat16):
    level = level_of(key, dims, split, -0.22, 0.18) if split else 1.0
    array = jax.random.normal(key, dims, jnp.float32) * spread * level
    return jnp.minimum(jnp.maximum(array, -limit), limit).astype(held_as)


def gaussian_with(key, dims, deviation, bound, shards, heavy, kind=jnp.bfloat16):
    drawn = deviation * jax.random.normal(key, dims, jnp.float32)
    if shards:
        drawn = drawn * level_of(key, dims, shards, -0.22, 0.18)
    return jnp.clip(raised(drawn, jax.random.fold_in(key, 3), *heavy), -bound, bound).astype(kind)


def setup_inputs(seed: int = 0) -> dict:
    arg_keys = jax.random.split(jax.random.key(seed), 6)
    audio_feats = gaussian_with(arg_keys[0], (CLIPS, L0, C), 1.0, 24.0, ((0, 256),), (0, 2, 256, 6.0))
    conv_weight = gaussian(arg_keys[1], (LAYERS, 3, C, C), (3 * C) ** -0.5, 0.15625)
    head_weight = gaussian(arg_keys[2], (NODES, C), C ** -0.5, 0.25, ((0, 16),))
    clip_owner_keys = jax.random.split(jax.random.fold_in(arg_keys[3], 1), CLIPS // CL_DEV)
    clip_owner_turns = jax.random.permutation(jax.random.fold_in(arg_keys[3], 3), CLIPS // CL_DEV)
    clip_owner = jax.vmap(lambda own, number: deal_out(jax.random.fold_in(arg_keys[3], 2), own, number, CL_DEV, N_LEAF, TOP, CAP, 2))(clip_owner_keys, clip_owner_turns).reshape((CLIPS, TOP))
    node_ids = set_ends(jax.random.randint(arg_keys[4], (CLIPS, TOP, NPAIR), 0, NODE_OWN), jax.random.fold_in(arg_keys[4], 1), 0, NODE_OWN - 1).astype(jnp.int32)
    return {"audio_feats": audio_feats, "conv_weight": conv_weight, "head_weight": head_weight, "clip_owner": clip_owner, "node_ids": node_ids}


inv_root_two = 0.7071067811865476
inv_root_two_pi = 0.3989422804014327


def gelu_value(value):
    return 0.5 * value * (1.0 + lax.erf(value * inv_root_two))


def gelu_slope(value):
    return 0.5 * (1.0 + lax.erf(value * inv_root_two)) + value * jnp.exp(-0.5 * value * value) * inv_root_two_pi


def reference(audio_feats, conv_weight, head_weight, clip_owner, node_ids):
    clip_count = audio_feats.shape[0]
    activation = audio_feats
    layer_inputs = []
    pre_list = []
    for layer_index in range(LAYERS):
        length = activation.shape[1] // 3
        folded = activation.reshape(clip_count * length, 3 * C)
        pre_act = jnp.dot(folded, conv_weight[layer_index].reshape(3 * C, C), preferred_element_type=jnp.float32)
        layer_inputs.append(folded)
        pre_list.append(pre_act)
        if layer_index + 1 < LAYERS:
            activation = gelu_value(pre_act).astype(jnp.bfloat16).reshape(clip_count, length, C)
    final_pre = pre_list[-1].reshape(clip_count, 3, C)
    embedding = jnp.mean(gelu_value(final_pre), axis=1).astype(jnp.bfloat16)

    labels = (jnp.arange(NPAIR) < NPOS).astype(jnp.float32)
    block_count = clip_count // CL_DEV

    def block_step(head_total, block_index):
        start = (block_index * CL_DEV).astype(jnp.int32)
        emb_block = lax.dynamic_slice_in_dim(embedding, start, CL_DEV, 0).astype(jnp.float32)
        owner_block = lax.dynamic_slice_in_dim(clip_owner, start, CL_DEV, 0)
        node_block = lax.dynamic_slice_in_dim(node_ids, start, CL_DEV, 0)
        global_node = (owner_block[:, :, None] * NODE_OWN + node_block).astype(jnp.int32)
        node_rows = head_weight[global_node].astype(jnp.float32)
        logits = jnp.einsum("btpc,bc->btp", node_rows, emb_block, precision=lax.Precision.HIGHEST)
        dlogit = jax.nn.sigmoid(logits) - labels
        route_grad = jnp.einsum("btp,btpc->btc", dlogit, node_rows, precision=lax.Precision.HIGHEST).astype(jnp.bfloat16)
        clip_grad = jnp.sum(route_grad.astype(jnp.float32), axis=1)
        terms = dlogit[:, :, :, None] * emb_block[:, None, None, :]
        head_total = head_total + jax.ops.segment_sum(terms.reshape(-1, C), global_node.reshape(-1), num_segments=NODES)
        return head_total, clip_grad

    head_total, clip_grads = lax.scan(block_step, jnp.zeros((NODES, C), jnp.float32), jnp.arange(block_count, dtype=jnp.int32))
    head_grad = head_total.astype(jnp.bfloat16)
    clip_grad = clip_grads.reshape(clip_count, C)

    upstream = ((clip_grad[:, None, :] / 3.0) * gelu_slope(final_pre)).astype(jnp.bfloat16).reshape(clip_count * 3, C)
    grad_list = []
    for layer_index in range(LAYERS - 1, -1, -1):
        weight_flat = conv_weight[layer_index].reshape(3 * C, C)
        grad_list = [jnp.dot(layer_inputs[layer_index].T, upstream, preferred_element_type=jnp.float32)] + grad_list
        if layer_index > 0:
            back_prop = jnp.dot(upstream, weight_flat.T, preferred_element_type=jnp.float32)
            back_prop = back_prop.reshape(-1, C)
            upstream = (back_prop * gelu_slope(pre_list[layer_index - 1])).astype(jnp.bfloat16)
    conv_grad = jnp.stack(grad_list).reshape(LAYERS, 3, C, C).astype(jnp.bfloat16)
    return conv_grad, head_grad
```

```python
import functools

import jax
import jax.numpy as jnp
from jax import lax
from jax.experimental import pallas as pl
from jax.experimental.pallas import tpu as pltpu
from jax.sharding import PartitionSpec as P

MESH = pl.DeviceIdType.MESH
F32 = jnp.float32
BF16 = jnp.bfloat16
INV_ROOT_TWO = 0.7071067811865476
INV_ROOT_TWO_PI = 0.3989422804014327

NT = (((1,), (1,)), ((), ()))
TN = (((0,), (0,)), ((), ()))


def dot(a, b, dims=(((1,), (0,)), ((), ()))):
    return lax.dot_general(a, b, dims, preferred_element_type=F32)


def gelu_pair(value):
    half = 0.5 * (1.0 + lax.erf(value * INV_ROOT_TWO))
    bell = jnp.exp(-0.5 * value * value) * INV_ROOT_TWO_PI
    return value * half, half + value * bell


def bytes_wait(ref, sem):
    pltpu.make_async_copy(ref, ref, sem).wait()


def kernel(
    nd, nl, chunk, groups,
    a_hbm, w_hbm, h_hbm, own_ref, node_ref,
    conv_ref, head_ref,
    a_v, w_v, h_v, ht_v, p_v, a1_v, sl0_v, sl1_v, emb_v, d_v,
    nsend_v, nrecv_v, esend_v, erecv_v, call_v, cpos_v, st_v, gsend_v, grecv_v,
    hsend_v, hrecv_v, u1_v, u0_v, wown_v, wsend_v, wrecv_v, dsend_v, drecv_v,
    g_v, zsend_v, zrecv_v, zsum_v,
    load_sem, a_sem, n_sem, e_sem, erecv_sem, g_sem, h_sem, csend_sem, crecv_sem,
    dsend_sem, drecv_sem, zsend_sem, zrecv_sem,
):
    me = lax.axis_index("leaf")
    mine = lax.axis_index("dp")
    core = lax.rem(me, 2)
    sibling = me + 1 - 2 * core
    clips = emb_v.shape[0]
    chan = emb_v.shape[1]
    cap = esend_v.shape[0] // nl
    slots = nl * cap
    nodes = h_v.shape[0]
    pairs = node_ref.shape[1]
    half = chan // 2
    span = nodes // nd
    rows_dp = chan // nd
    cols_leaf = chan // nl
    steps = clips // chunk

    load_w0 = pltpu.make_async_copy(w_hbm.at[0], w_v.at[0], load_sem.at[0])
    load_w1 = pltpu.make_async_copy(w_hbm.at[1], w_v.at[1], load_sem.at[1])
    load_h = pltpu.make_async_copy(h_hbm, h_v, load_sem.at[2])

    def load_a(i):
        part = pl.ds(pl.multiple_of(i * chunk, chunk), chunk)
        return pltpu.make_async_copy(a_hbm.at[:, :, part], a_v.at[:, :, part], a_sem.at[i])

    load_w0.start()
    for i in range(steps):
        load_a(i).start()
    load_w1.start()
    load_h.start()

    barrier = pltpu.get_barrier_semaphore()

    @pl.loop(1, nl)
    def _(i):
        pl.semaphore_signal(
            barrier, inc=1, device_id={"leaf": lax.rem(me + i, nl)}, device_id_type=MESH
        )

    @pl.loop(1, nd)
    def _(i):
        pl.semaphore_signal(
            barrier, inc=1, device_id={"dp": lax.rem(mine + i, nd)}, device_id_type=MESH
        )

    owner_iota = lax.broadcasted_iota(jnp.int32, (nl, clips), 0)
    before = (
        lax.broadcasted_iota(jnp.int32, (clips, clips), 0)
        < lax.broadcasted_iota(jnp.int32, (clips, clips), 1)
    ).astype(F32).astype(BF16)
    slot_iota = lax.broadcasted_iota(jnp.int32, (slots, clips), 0)
    base = jnp.zeros((nl, 1), F32)
    spots = []
    lists = jnp.zeros((slots, 128), F32)
    for r in range(2):
        hit = (own_ref[r : r + 1, :] == owner_iota).astype(F32)
        rank = dot(hit.astype(BF16), before) + base
        base = base + jnp.sum(hit, axis=1, keepdims=True)
        place = jnp.sum(hit * (rank + (owner_iota * cap).astype(F32)), axis=0, keepdims=True)
        spot = (slot_iota == place.astype(jnp.int32)).astype(F32).astype(BF16)
        spots.append(spot)
        ident = node_ref[r] + 1
        upper = (ident >> 7).astype(F32)
        lower = (ident & 127).astype(F32)
        pad = jnp.zeros((128 - pairs, clips), F32)
        upper = jnp.concatenate([upper, pad], axis=0).astype(BF16)
        lower = jnp.concatenate([lower, pad], axis=0).astype(BF16)
        lists = lists + dot(spot, upper, NT) * 128.0 + dot(spot, lower, NT)
    d_v[...] = spots[0] + spots[1]
    nsend_v[...] = lists - 1.0

    pl.semaphore_wait(barrier, nl - 1 + nd - 1)

    def block(i):
        return pl.ds(pl.multiple_of(i * cap, cap), cap)

    per = nl // groups
    group = me // per
    inside = lax.rem(me, per)

    def peers(t):
        if t == 0:
            return [group * per + lax.rem(inside + o, per) for o in range(1, per)]
        return [lax.rem(group + t, groups) * per + o for o in range(per)]

    nrecv_v[block(me), :] = nsend_v[block(me), :]

    @pl.loop(1, nl)
    def _(i):
        to = lax.rem(me + i, nl)
        pltpu.make_async_remote_copy(
            nsend_v.at[block(to)], nrecv_v.at[block(me)], n_sem.at[0], n_sem.at[1],
            device_id={"leaf": to}, device_id_type=MESH,
        ).start()

    load_w0.wait()

    @pl.loop(0, steps)
    def _(i):
        load_a(i).wait()
        part = pl.ds(pl.multiple_of(i * chunk, chunk), chunk)
        folded = jnp.concatenate(
            [a_v[:, k, part, :].reshape(9 * chunk, chan) for k in range(3)], axis=1
        )
        p_v[...] = dot(folded, w_v[0]).reshape(9, chunk, chan)

        @pl.loop(0, 9)
        def _(j):
            act, slope = gelu_pair(p_v[j])
            a1_v[j, part, :] = act.astype(BF16)
            sl0_v[j, part, :] = slope

    load_w1.wait()

    @pl.loop(0, 3)
    def _(j):
        folded = jnp.concatenate([a1_v[3 * j + k] for k in range(3)], axis=1)
        sl1_v[j] = dot(folded, w_v[1])

    @pl.loop(0, steps)
    def _(i):
        part = pl.ds(pl.multiple_of(i * chunk, chunk), chunk)
        total = jnp.zeros((chunk, chan), F32)
        for j in range(3):
            act, slope = gelu_pair(sl1_v[j, part, :])
            sl1_v[j, part, :] = slope
            total = total + act
        emb_v[part, :] = (total * (1.0 / 3.0)).astype(BF16)

    esend_v[...] = dot(d_v[...], emb_v[...]).astype(BF16)
    erecv_v[block(me), :] = esend_v[block(me), :]

    def emb_copy(to, source):
        return pltpu.make_async_remote_copy(
            esend_v.at[block(to)], erecv_v.at[block(source)], e_sem.at[0],
            erecv_sem.at[source], device_id={"leaf": to}, device_id_type=MESH,
        )

    for t in range(groups):
        for to in peers(t):
            emb_copy(to, me).start()

    load_h.wait()
    piece = nodes // 4

    for i in range(4):
        ht_v[:, i * piece : (i + 1) * piece] = h_v[i * piece : (i + 1) * piece, :].T

    bytes_wait(nsend_v.at[pl.ds(0, (nl - 1) * cap)], n_sem.at[0])
    bytes_wait(nrecv_v.at[pl.ds(0, (nl - 1) * cap)], n_sem.at[1])
    node_iota = lax.broadcasted_iota(jnp.int32, (16, nodes), 1).astype(F32)

    @pl.loop(0, slots // 16)
    def _(i):
        part = pl.ds(pl.multiple_of(i * 16, 16), 16)
        named = nrecv_v[part, :]
        tally = jnp.zeros((16, nodes), F32)
        for q in range(pairs):
            weight = 17.0 if q < pairs // 2 else 1.0
            tally = tally + jnp.where(named[:, q : q + 1] == node_iota, weight, 0.0)
        positive = jnp.floor(tally * (1.0 / 16.0))
        cpos_v[part, :] = positive.astype(BF16)
        call_v[part, :] = (tally - 16.0 * positive).astype(BF16)

    lanes = nodes // 4
    for t in range(groups):
        source_group = lax.rem(group + groups - t, groups)
        for i in range(per):
            source = source_group * per + i
            if t == 0:

                @pl.when(source != me)
                def _():
                    emb_copy(source, source).wait_recv()
            else:
                emb_copy(source, source).wait_recv()
        start = pl.multiple_of(source_group * (per * cap), per * cap)
        rows = pl.ds(start, per * cap)
        emb = erecv_v[rows, :]

        @pl.loop(0, 4)
        def _(n):
            cols = pl.ds(pl.multiple_of(n * lanes, lanes), lanes)
            score = dot(emb, ht_v[:, cols])
            sig = 0.5 * jnp.tanh(0.5 * score) + 0.5
            st_v[rows, cols] = (
                sig * call_v[rows, cols].astype(F32) - cpos_v[rows, cols].astype(F32)
            ).astype(BF16)

        gsend_v[rows, :] = dot(st_v[rows, :], h_v[...]).astype(BF16)
        if t == 0:
            grecv_v[block(me), :] = gsend_v[block(me), :]
            back = [group * per + lax.rem(inside + o, per) for o in range(1, per)]
        else:
            back = [source_group * per + o for o in range(per)]
        for to in back:
            pltpu.make_async_remote_copy(
                gsend_v.at[block(to)], grecv_v.at[block(me)], g_sem.at[0], g_sem.at[1],
                device_id={"leaf": to}, device_id_type=MESH,
            ).start()

    @pl.loop(0, nd)
    def _(i):
        to = lax.rem(mine + i, nd)
        cols = pl.ds(pl.multiple_of(to * span, span), span)
        hsend_v[to] = dot(st_v[:, cols], erecv_v[...], TN).astype(BF16)

        @pl.when(i > 0)
        def _():
            pltpu.make_async_remote_copy(
                hsend_v.at[to], hrecv_v.at[mine], h_sem.at[0], h_sem.at[1],
                device_id={"dp": to}, device_id_type=MESH,
            ).start()

    hrecv_v[mine] = hsend_v[mine]

    bytes_wait(grecv_v.at[pl.ds(0, (nl - 1) * cap)], g_sem.at[1])
    clip_grad = dot(d_v[...], grecv_v[...], TN) * (1.0 / 3.0)
    for j in range(3):
        u1_v[j] = (clip_grad * sl1_v[j]).astype(BF16)

    def leave(step, grad):
        low, high = grad[:, :half], grad[:, half:]
        wown_v[step] = jnp.where(core == 0, low, high)
        wsend_v[step] = jnp.where(core == 0, high, low).astype(BF16)
        core_copy(step).start()

    def core_copy(step):
        return pltpu.make_async_remote_copy(
            wsend_v.at[step], wrecv_v.at[step], csend_sem.at[step], crecv_sem.at[step],
            device_id={"leaf": sibling}, device_id_type=MESH,
        )

    def spread(step):
        core_copy(step).wait_recv()
        both = (wown_v[step] + wrecv_v[step].astype(F32)).astype(BF16)
        dsend_v[step] = both.reshape(nd, rows_dp, half)
        drecv_v[step, mine] = dsend_v[step, mine]

        @pl.loop(1, nd)
        def _(i):
            to = lax.rem(mine + i, nd)
            pltpu.make_async_remote_copy(
                dsend_v.at[step, to], drecv_v.at[step, mine], dsend_sem.at[step],
                drecv_sem.at[step], device_id={"dp": to}, device_id_type=MESH,
            ).start()

    @pl.loop(0, 3)
    def _(k):
        left = jnp.concatenate([a1_v[3 * j + k] for j in range(3)], axis=0)
        leave(3 + k, dot(left, u1_v[...].reshape(3 * clips, chan), TN))

    @pl.loop(0, 3)
    def _(k):
        taps = w_v[1, pl.ds(pl.multiple_of(k * chan, chan), chan), :]
        for j in range(3):
            u0_v[3 * j + k] = (dot(u1_v[j], taps, NT) * sl0_v[3 * j + k]).astype(BF16)

    @pl.loop(0, 3)
    def _(k):
        spread(3 + k)

    @pl.loop(0, 3)
    def _(k):
        left = a_v[:, k].reshape(9 * clips, chan)
        leave(k, dot(left, u0_v[...].reshape(9 * clips, chan), TN))

    @pl.loop(0, 3)
    def _(k):
        spread(k)

    bytes_wait(hrecv_v.at[pl.ds(0, nd - 1)], h_sem.at[1])

    @pl.loop(0, span // 16)
    def _(i):
        part = pl.ds(pl.multiple_of(i * 16, 16), 16)
        total = hrecv_v[0, part, :].astype(F32)
        for d in range(1, nd):
            total = total + hrecv_v[d, part, :].astype(F32)
        head_ref[part, :] = total.astype(BF16)

    filled = 6 * rows_dp
    if g_v.shape[0] > filled:
        g_v[filled:, :] = jnp.zeros((g_v.shape[0] - filled, half), F32)

    def gather_step(step):
        bytes_wait(drecv_v.at[step, pl.ds(0, nd - 1)], drecv_sem.at[step])
        total = drecv_v[step, 0].astype(F32)
        for d in range(1, nd):
            total = total + drecv_v[step, d].astype(F32)
        g_v[pl.ds(pl.multiple_of(step * rows_dp, rows_dp), rows_dp), :] = total

    @pl.loop(0, 3)
    def _(k):
        gather_step(3 + k)

    @pl.loop(0, 3)
    def _(k):
        gather_step(k)

    zsend_v[...] = g_v[...].T.astype(BF16).reshape(nl // 2, cols_leaf, g_v.shape[0])
    my_z = me // 2
    for i in range(nl // 2):
        to = core * (nl // 2) + i

        @pl.when(to == me)
        def _():
            zrecv_v[my_z] = zsend_v[i]

        @pl.when(to != me)
        def _():
            pltpu.make_async_remote_copy(
                zsend_v.at[i], zrecv_v.at[my_z], zsend_sem.at[i], zrecv_sem.at[my_z],
                device_id={"leaf": to}, device_id_type=MESH,
            ).start()

    giver = me // (nl // 2)
    zsum_v[...] = jnp.zeros(zsum_v.shape, F32)
    for z in range(nl // 2):

        @pl.when(2 * z + giver != me)
        def _():
            pltpu.make_async_remote_copy(
                zsend_v.at[z], zrecv_v.at[z], zsend_sem.at[z], zrecv_sem.at[z],
                device_id={"leaf": sibling}, device_id_type=MESH,
            ).wait_recv()

    total = zrecv_v[0].astype(F32)
    for z in range(1, nl // 2):
        total = total + zrecv_v[z].astype(F32)
    zsum_v[0:cols_leaf, :] = total
    final = zsum_v[...].T[:filled, :cols_leaf]
    conv_ref[...] = final.reshape(2, 3, rows_dp, cols_leaf).astype(BF16)

    bytes_wait(esend_v.at[pl.ds(0, (nl - 1) * cap)], e_sem.at[0])
    bytes_wait(gsend_v.at[pl.ds(0, (nl - 1) * cap)], g_sem.at[0])
    bytes_wait(hsend_v.at[pl.ds(0, nd - 1)], h_sem.at[0])

    @pl.loop(0, 6)
    def _(step):
        core_copy(step).wait_send()
        bytes_wait(dsend_v.at[step, pl.ds(0, nd - 1)], dsend_sem.at[step])

    for i in range(nl // 2):

        @pl.when(core * (nl // 2) + i != me)
        def _():
            pltpu.make_async_remote_copy(
                zsend_v.at[i], zrecv_v.at[my_z], zsend_sem.at[i], zrecv_sem.at[my_z],
                device_id={"leaf": sibling}, device_id_type=MESH,
            ).wait_send()


def body(audio, weight, head_weight, clip_owner, node_ids, *, nd, nl):
    clips, length, chan = audio.shape
    nodes = head_weight.shape[0]
    routes = clip_owner.shape[1]
    pairs = node_ids.shape[2]
    cap = 2 * clips * routes // nl
    slots = nl * cap
    half = chan // 2
    rows_dp, cols_leaf = chan // nd, chan // nl
    filled = -(-6 * rows_dp // 128) * 128
    chunk = 48
    groups = 4 if nl >= 8 else 2
    steps = clips // chunk
    a = jnp.transpose(audio, (1, 0, 2)).reshape(length // 3, 3, clips, chan)
    w = weight.reshape(2, 3 * chan, chan)
    own = jnp.transpose(clip_owner, (1, 0))
    ids = jnp.transpose(node_ids, (1, 2, 0))
    vm = pltpu.VMEM
    dma = pltpu.SemaphoreType.DMA
    scratch = [
        vm((9, 3, clips, chan), BF16),
        vm((2, 3 * chan, chan), BF16),
        vm((nodes, chan), BF16),
        vm((chan, nodes), BF16),
        vm((9, chunk, chan), F32),
        vm((9, clips, chan), BF16),
        vm((9, clips, chan), F32),
        vm((3, clips, chan), F32),
        vm((clips, chan), BF16),
        vm((slots, clips), BF16),
        vm((slots, 128), F32),
        vm((slots, 128), F32),
        vm((slots, chan), BF16),
        vm((slots, chan), BF16),
        vm((slots, nodes), BF16),
        vm((slots, nodes), BF16),
        vm((slots, nodes), BF16),
        vm((slots, chan), BF16),
        vm((slots, chan), BF16),
        vm((nd, nodes // nd, chan), BF16),
        vm((nd, nodes // nd, chan), BF16),
        vm((3, clips, chan), BF16),
        vm((9, clips, chan), BF16),
        vm((6, chan, half), F32),
        vm((6, chan, half), BF16),
        vm((6, chan, half), BF16),
        vm((6, nd, rows_dp, half), BF16),
        vm((6, nd, rows_dp, half), BF16),
        vm((filled, half), F32),
        vm((nl // 2, cols_leaf, filled), BF16),
        vm((nl // 2, cols_leaf, filled), BF16),
        vm((max(128, cols_leaf), filled), F32),
        dma((3,)), dma((steps,)), dma((2,)), dma((1,)), dma((nl,)), dma((2,)), dma((2,)),
        dma((6,)), dma((6,)), dma((6,)), dma((6,)), dma((nl // 2,)), dma((nl // 2,)),
    ]
    whole = pl.BlockSpec(memory_space=pltpu.VMEM)
    far = pl.BlockSpec(memory_space=pl.ANY)
    return pl.pallas_call(
        functools.partial(kernel, nd, nl, chunk, groups),
        out_shape=(
            jax.ShapeDtypeStruct((2, 3, rows_dp, cols_leaf), BF16),
            jax.ShapeDtypeStruct((nodes // nd, chan), BF16),
        ),
        in_specs=[far, far, far, whole, whole],
        out_specs=(whole, whole),
        scratch_shapes=scratch,
        compiler_params=pltpu.CompilerParams(
            collective_id=0, has_side_effects=True, vmem_limit_bytes=62914560
        ),
    )(a, w, head_weight, own, ids)


def solution(mesh):
    placed = (
        P(("dp", "leaf"), None, None),
        P(),
        P("leaf", None),
        P(("dp", "leaf"), None),
        P(("dp", "leaf"), None, None),
    )
    return jax.shard_map(
        functools.partial(body, nd=mesh.shape["dp"], nl=mesh.shape["leaf"]),
        mesh=mesh,
        in_specs=placed,
        out_specs=(P(None, None, "dp", "leaf"), P(("leaf", "dp"), None)),
        check_vma=False,
    )
```

```python
import functools
import math

import jax
import jax.numpy as jnp
from jax import lax
from jax.experimental import pallas as pl
from jax.experimental.pallas import tpu as pltpu
from jax.sharding import PartitionSpec as P

MESH = pl.DeviceIdType.MESH
F32 = jnp.float32
BF16 = jnp.bfloat16
INV_ROOT_TWO = 0.7071067811865476
INV_ROOT_TWO_PI = 0.3989422804014327

NT = (((1,), (1,)), ((), ()))
TN = (((0,), (0,)), ((), ()))


def dot(a, b, dims=(((1,), (0,)), ((), ()))):
    return lax.dot_general(a, b, dims, preferred_element_type=F32)


def gelu_pair(value):
    half = 0.5 * (1.0 + lax.erf(value * INV_ROOT_TWO))
    bell = jnp.exp(-0.5 * value * value) * INV_ROOT_TWO_PI
    return value * half, half + value * bell


def bytes_wait(ref, sem):
    pltpu.make_async_copy(ref, ref, sem).wait()


def kernel(
    ny, nx, nl, chunk, groups,
    a_hbm, w_hbm, h_hbm, own_ref, node_ref,
    conv_ref, head_ref,
    a_v, w_v, h_v, ht_v, pa_v, pb_v, a1_v, sl0_v, sl1_v, emb_v, d_v,
    nsend_v, nrecv_v, esend_v, erecv_v, call_v, cpos_v, st_v, gsend_v, grecv_v,
    hsend_v, hone_v, hmid_v, htwo_v, u1_v, u0_v, wown_v, wsend_v, wrecv_v,
    dsend_v, done_v, dmid_v, dtwo_v,
    g_v, zsend_v, zrecv_v, zsum_v,
    load_sem, a_sem, n_sem, e_sem, erecv_sem, g_sem, h_sem, csend_sem, crecv_sem,
    d_sem, zsend_sem, zrecv_sem,
):
    me = lax.axis_index("leaf")
    mine = lax.axis_index("dp")
    core = lax.rem(me, 2)
    sibling = me + 1 - 2 * core
    clips = emb_v.shape[0]
    chan = emb_v.shape[1]
    cap = esend_v.shape[0] // nl
    slots = nl * cap
    nodes = h_v.shape[0]
    pairs = node_ref.shape[1]
    nd = ny * nx
    my_y, my_x = mine // nx, lax.rem(mine, nx)
    half = chan // 2
    span = nodes // nd
    rows_dp = chan // nd
    cols_leaf = chan // nl
    steps = clips // chunk

    load_w0 = pltpu.make_async_copy(w_hbm.at[0], w_v.at[0], load_sem.at[0])
    load_w1 = pltpu.make_async_copy(w_hbm.at[1], w_v.at[1], load_sem.at[1])
    load_h = pltpu.make_async_copy(h_hbm, h_v, load_sem.at[2])

    def load_a(i):
        part = pl.ds(pl.multiple_of(i * chunk, chunk), chunk)
        return pltpu.make_async_copy(a_hbm.at[:, :, part], a_v.at[:, :, part], a_sem.at[i])

    load_w0.start()
    for i in range(steps):
        load_a(i).start()
    load_w1.start()
    load_h.start()

    barrier = pltpu.get_barrier_semaphore()

    @pl.loop(1, nl)
    def _(i):
        pl.semaphore_signal(
            barrier, inc=1, device_id={"leaf": lax.rem(me + i, nl)}, device_id_type=MESH
        )

    @pl.loop(1, nd)
    def _(i):
        pl.semaphore_signal(
            barrier, inc=1, device_id={"dp": lax.rem(mine + i, nd)}, device_id_type=MESH
        )

    owner_iota = lax.broadcasted_iota(jnp.int32, (nl, clips), 0)
    before = (
        lax.broadcasted_iota(jnp.int32, (clips, clips), 0)
        < lax.broadcasted_iota(jnp.int32, (clips, clips), 1)
    ).astype(F32).astype(BF16)
    slot_iota = lax.broadcasted_iota(jnp.int32, (slots, clips), 0)
    list_iota = lax.broadcasted_iota(jnp.int32, (nl * 128, clips), 0)
    base = jnp.zeros((nl, 1), F32)
    spots = []
    lists = jnp.zeros((2 * pairs, nl * 128), F32)
    for r in range(2):
        hit = (own_ref[r : r + 1, :] == owner_iota).astype(F32)
        rank = dot(hit.astype(BF16), before) + base
        base = base + jnp.sum(hit, axis=1, keepdims=True)

        def place(stride):
            spot = jnp.sum(
                hit * (rank + (owner_iota * stride).astype(F32)), axis=0, keepdims=True
            )
            return spot.astype(jnp.int32)

        spots.append((slot_iota == place(cap)).astype(F32).astype(BF16))
        wide = (list_iota == place(128)).astype(F32).astype(BF16)
        ident = node_ref[r] + 1
        parts = jnp.concatenate([ident >> 7, ident & 127], axis=0).astype(F32).astype(BF16)
        lists = lists + dot(parts, wide, NT)
    d_v[...] = spots[0] + spots[1]
    for o in range(nl):
        nsend_v[o] = lists[:, o * 128 : (o + 1) * 128].astype(BF16)

    def block(i):
        return pl.ds(pl.multiple_of(i * cap, cap), cap)

    per = nl // groups
    group = me // per
    inside = lax.rem(me, per)

    def peers(t):
        if t == 0:
            return [group * per + lax.rem(inside + o, per) for o in range(1, per)]
        return [lax.rem(group + t, groups) * per + o for o in range(per)]

    load_w0.wait()

    stage = [pa_v, pb_v]

    def multiply(i):
        load_a(i).wait()
        part = pl.ds(i * chunk, chunk)
        folded = jnp.concatenate(
            [a_v[:, k, part, :].reshape(9 * chunk, chan) for k in range(3)], axis=1
        )
        stage[i % 2][...] = dot(folded, w_v[0]).reshape(9, chunk, chan)

    def activate(i):
        part = pl.ds(i * chunk, chunk)

        @pl.loop(0, 9, unroll=True)
        def _(j):
            act, slope = gelu_pair(stage[i % 2][j])
            a1_v[j, part, :] = act.astype(BF16)
            sl0_v[j, part, :] = slope

    multiply(0)
    for i in range(steps):
        if i + 1 < steps:
            multiply(i + 1)
        activate(i)

    load_w1.wait()

    @pl.loop(0, 3)
    def _(j):
        folded = jnp.concatenate([a1_v[3 * j + k] for k in range(3)], axis=1)
        sl1_v[j] = dot(folded, w_v[1])

    @pl.loop(0, steps)
    def _(i):
        part = pl.ds(pl.multiple_of(i * chunk, chunk), chunk)
        total = jnp.zeros((chunk, chan), F32)
        for j in range(3):
            act, slope = gelu_pair(sl1_v[j, part, :])
            sl1_v[j, part, :] = slope
            total = total + act
        emb_v[part, :] = (total * (1.0 / 3.0)).astype(BF16)

    pl.semaphore_wait(barrier, nl - 1 + nd - 1)
    nrecv_v[me] = nsend_v[me]

    @pl.loop(1, nl)
    def _(i):
        to = lax.rem(me + i, nl)
        pltpu.make_async_remote_copy(
            nsend_v.at[to], nrecv_v.at[me], n_sem.at[0], n_sem.at[1],
            device_id={"leaf": to}, device_id_type=MESH,
        ).start()

    esend_v[...] = dot(d_v[...], emb_v[...]).astype(BF16)
    erecv_v[block(me), :] = esend_v[block(me), :]

    def emb_copy(to, source):
        return pltpu.make_async_remote_copy(
            esend_v.at[block(to)], erecv_v.at[block(source)], e_sem.at[0],
            erecv_sem.at[source], device_id={"leaf": to}, device_id_type=MESH,
        )

    for t in range(groups):
        for to in peers(t):
            emb_copy(to, me).start()

    load_h.wait()
    piece = nodes // 4

    for i in range(4):
        ht_v[:, i * piece : (i + 1) * piece] = h_v[i * piece : (i + 1) * piece, :].T

    bytes_wait(nsend_v.at[pl.ds(0, nl - 1)], n_sem.at[0])
    bytes_wait(nrecv_v.at[pl.ds(0, nl - 1)], n_sem.at[1])
    node_iota = lax.broadcasted_iota(jnp.int32, (16, nodes), 1).astype(F32)

    @pl.loop(0, nl)
    def _(o):
        parts = nrecv_v[o].astype(F32)
        named = (parts[:pairs] * 128.0 + parts[pairs:] - 1.0).T
        for i in range(cap // 16):
            part = pl.ds(pl.multiple_of(o * cap + i * 16, 16), 16)
            tally = jnp.zeros((16, nodes), F32)
            for q in range(pairs):
                weight = 17.0 if q < pairs // 2 else 1.0
                ident = named[i * 16 : (i + 1) * 16, q : q + 1]
                tally = tally + jnp.where(ident == node_iota, weight, 0.0)
            positive = jnp.floor(tally * (1.0 / 16.0))
            cpos_v[part, :] = positive.astype(BF16)
            call_v[part, :] = (tally - 16.0 * positive).astype(BF16)

    lanes = nodes // 4
    for t in range(groups):
        source_group = lax.rem(group + groups - t, groups)
        for i in range(per):
            source = source_group * per + i
            if t == 0:

                @pl.when(source != me)
                def _():
                    emb_copy(source, source).wait_recv()
            else:
                emb_copy(source, source).wait_recv()
        start = pl.multiple_of(source_group * (per * cap), per * cap)
        rows = pl.ds(start, per * cap)
        emb = erecv_v[rows, :]

        @pl.loop(0, 4)
        def _(n):
            cols = pl.ds(pl.multiple_of(n * lanes, lanes), lanes)
            score = dot(emb, ht_v[:, cols])
            sig = 0.5 * jnp.tanh(0.5 * score) + 0.5
            st_v[rows, cols] = (
                sig * call_v[rows, cols].astype(F32) - cpos_v[rows, cols].astype(F32)
            ).astype(BF16)

        gsend_v[rows, :] = dot(st_v[rows, :], h_v[...]).astype(BF16)
        if t == 0:
            grecv_v[block(me), :] = gsend_v[block(me), :]
            back = [group * per + lax.rem(inside + o, per) for o in range(1, per)]
        else:
            back = [source_group * per + o for o in range(per)]
        for to in back:
            pltpu.make_async_remote_copy(
                gsend_v.at[block(to)], grecv_v.at[block(me)], g_sem.at[0], g_sem.at[1],
                device_id={"leaf": to}, device_id_type=MESH,
            ).start()

    low_rows, high_rows = pl.ds(0, span // 2), pl.ds(span // 2, span // 2)

    def over_x(o):
        return {"dp": my_y * nx + lax.rem(my_x + o, nx)}

    def over_y(o):
        return {"dp": lax.rem(my_y + o, ny) * nx + my_x}

    def send(source, target, sems, device):
        pltpu.make_async_remote_copy(
            source, target, sems.at[0], sems.at[1], device_id=device, device_id_type=MESH
        ).start()

    for o in range(1, ny + 1):
        y = lax.rem(my_y + o, ny)
        cols = pl.ds(pl.multiple_of(y * nx * span, nx * span), nx * span)
        terms = dot(st_v[:, cols], erecv_v[...], TN).astype(BF16)
        hsend_v[y] = terms.reshape(nx, span, chan)
        if o < ny:
            send(hsend_v.at[y, :, high_rows], hone_v.at[1, o - 1], h_sem.at[1], over_y(o))
    for o in range(1, nx):
        x = lax.rem(my_x + o, nx)
        send(hsend_v.at[:, x, low_rows], hone_v.at[0, o - 1], h_sem.at[0], over_x(o))

    bytes_wait(hone_v.at[1], h_sem.at[1, 1])
    bytes_wait(hone_v.at[0], h_sem.at[0, 1])
    strip = 32

    @pl.loop(0, ny)
    def _(i):
        for at in range(0, span // 2, strip):
            part = pl.ds(at, strip)
            total = hsend_v[i, my_x, part, :].astype(F32)
            for o in range(nx - 1):
                total = total + hone_v[0, o, i, part, :].astype(F32)
            hmid_v[0, i, part, :] = total.astype(BF16)
            total = hsend_v[my_y, i, pl.ds(span // 2 + at, strip), :].astype(F32)
            for o in range(ny - 1):
                total = total + hone_v[1, o, i, part, :].astype(F32)
            hmid_v[1, i, part, :] = total.astype(BF16)

    for o in range(1, ny):
        send(hmid_v.at[0, lax.rem(my_y + o, ny)], htwo_v.at[0, o - 1], h_sem.at[2], over_y(o))
        send(hmid_v.at[1, lax.rem(my_x + o, nx)], htwo_v.at[1, o - 1], h_sem.at[3], over_x(o))

    bytes_wait(grecv_v.at[pl.ds(0, (nl - 1) * cap)], g_sem.at[1])
    clip_grad = dot(d_v[...], grecv_v[...], TN) * (1.0 / 3.0)
    for j in range(3):
        u1_v[j] = (clip_grad * sl1_v[j]).astype(BF16)

    def leave(step, grad):
        low, high = grad[:, :half], grad[:, half:]
        wown_v[step] = jnp.where(core == 0, low, high)
        wsend_v[step] = jnp.where(core == 0, high, low).astype(BF16)
        core_copy(step).start()

    def core_copy(step):
        return pltpu.make_async_remote_copy(
            wsend_v.at[step], wrecv_v.at[step], csend_sem.at[step], crecv_sem.at[step],
            device_id={"leaf": sibling}, device_id_type=MESH,
        )

    part_rows = rows_dp // 2
    low_part, high_part = pl.ds(0, part_rows), pl.ds(part_rows, part_rows)

    def spread(step):
        core_copy(step).wait_recv()
        both = (wown_v[step] + wrecv_v[step].astype(F32)).astype(BF16)
        dsend_v[step] = both.reshape(ny, nx, rows_dp, half)
        for o in range(1, nx):
            x = lax.rem(my_x + o, nx)
            send(
                dsend_v.at[step, :, x, low_part], done_v.at[step, 0, o - 1],
                d_sem.at[step, 0], over_x(o),
            )
        for o in range(1, ny):
            y = lax.rem(my_y + o, ny)
            send(
                dsend_v.at[step, y, :, high_part], done_v.at[step, 1, o - 1],
                d_sem.at[step, 1], over_y(o),
            )

    def respread(step):
        bytes_wait(done_v.at[step, 0], d_sem.at[step, 0, 1])
        total = dsend_v[step, :, my_x, low_part, :].astype(F32)
        for o in range(nx - 1):
            total = total + done_v[step, 0, o].astype(F32)
        dmid_v[step, 0] = total.astype(BF16)
        bytes_wait(done_v.at[step, 1], d_sem.at[step, 1, 1])
        total = dsend_v[step, my_y, :, high_part, :].astype(F32)
        for o in range(ny - 1):
            total = total + done_v[step, 1, o].astype(F32)
        dmid_v[step, 1] = total.astype(BF16)
        for o in range(1, ny):
            send(
                dmid_v.at[step, 0, lax.rem(my_y + o, ny)], dtwo_v.at[step, 0, o - 1],
                d_sem.at[step, 2], over_y(o),
            )
            send(
                dmid_v.at[step, 1, lax.rem(my_x + o, nx)], dtwo_v.at[step, 1, o - 1],
                d_sem.at[step, 3], over_x(o),
            )

    def gather_step(step):
        for side, place in ((0, my_y), (1, my_x)):
            bytes_wait(dtwo_v.at[step, side], d_sem.at[step, 2 + side, 1])
            total = dmid_v[step, side, place].astype(F32)
            for o in range(ny - 1):
                total = total + dtwo_v[step, side, o].astype(F32)
            first = pl.multiple_of(step * rows_dp + side * part_rows, part_rows)
            g_v[pl.ds(first, part_rows), :] = total

    @pl.loop(0, 3)
    def _(k):
        left = jnp.concatenate([a1_v[3 * j + k] for j in range(3)], axis=0)
        leave(3 + k, dot(left, u1_v[...].reshape(3 * clips, chan), TN))

    @pl.loop(0, 3)
    def _(k):
        taps = w_v[1, pl.ds(pl.multiple_of(k * chan, chan), chan), :]
        for j in range(3):
            u0_v[3 * j + k] = (dot(u1_v[j], taps, NT) * sl0_v[3 * j + k]).astype(BF16)

    @pl.loop(0, 3)
    def _(k):
        spread(3 + k)

    @pl.loop(0, 3)
    def _(k):
        left = a_v[:, k].reshape(9 * clips, chan)
        leave(k, dot(left, u0_v[...].reshape(9 * clips, chan), TN))

        @pl.when(k > 0)
        def _():
            spread(k - 1)

    spread(2)

    filled = 6 * rows_dp
    if g_v.shape[0] > filled:
        g_v[filled:, :] = jnp.zeros((g_v.shape[0] - filled, half), F32)

    @pl.loop(0, 3)
    def _(k):
        respread(3 + k)

    @pl.loop(0, 3)
    def _(k):
        respread(k)

    for side, place in ((0, my_y), (1, my_x)):
        bytes_wait(htwo_v.at[side], h_sem.at[2 + side, 1])
        for at in range(0, span // 2, strip):
            part = pl.ds(at, strip)
            total = hmid_v[side, place, part, :].astype(F32)
            for o in range(ny - 1):
                total = total + htwo_v[side, o, part, :].astype(F32)
            head_ref[pl.ds(side * (span // 2) + at, strip), :] = total.astype(BF16)

    @pl.loop(0, 3)
    def _(k):
        gather_step(3 + k)

    @pl.loop(0, 3)
    def _(k):
        gather_step(k)

    zsend_v[...] = g_v[...].T.astype(BF16).reshape(nl // 2, cols_leaf, g_v.shape[0])
    my_z = me // 2
    for i in range(nl // 2):
        to = core * (nl // 2) + i

        @pl.when(to == me)
        def _():
            zrecv_v[my_z] = zsend_v[i]

        @pl.when(to != me)
        def _():
            pltpu.make_async_remote_copy(
                zsend_v.at[i], zrecv_v.at[my_z], zsend_sem.at[i], zrecv_sem.at[my_z],
                device_id={"leaf": to}, device_id_type=MESH,
            ).start()

    giver = me // (nl // 2)
    zsum_v[...] = jnp.zeros(zsum_v.shape, F32)
    for z in range(nl // 2):

        @pl.when(2 * z + giver != me)
        def _():
            pltpu.make_async_remote_copy(
                zsend_v.at[z], zrecv_v.at[z], zsend_sem.at[z], zrecv_sem.at[z],
                device_id={"leaf": sibling}, device_id_type=MESH,
            ).wait_recv()

    total = zrecv_v[0].astype(F32)
    for z in range(1, nl // 2):
        total = total + zrecv_v[z].astype(F32)
    zsum_v[0:cols_leaf, :] = total
    final = zsum_v[...].T[:filled, :cols_leaf]
    conv_ref[...] = final.reshape(2, 3, rows_dp, cols_leaf).astype(BF16)

    bytes_wait(esend_v.at[pl.ds(0, (nl - 1) * cap)], e_sem.at[0])
    bytes_wait(gsend_v.at[pl.ds(0, (nl - 1) * cap)], g_sem.at[0])
    for side in range(2):
        bytes_wait(hone_v.at[side], h_sem.at[side, 0])
        bytes_wait(htwo_v.at[side], h_sem.at[2 + side, 0])

    @pl.loop(0, 6)
    def _(step):
        core_copy(step).wait_send()
        for side in range(2):
            bytes_wait(done_v.at[step, side], d_sem.at[step, side, 0])
            bytes_wait(dtwo_v.at[step, side], d_sem.at[step, 2 + side, 0])

    for i in range(nl // 2):

        @pl.when(core * (nl // 2) + i != me)
        def _():
            pltpu.make_async_remote_copy(
                zsend_v.at[i], zrecv_v.at[my_z], zsend_sem.at[i], zrecv_sem.at[my_z],
                device_id={"leaf": sibling}, device_id_type=MESH,
            ).wait_send()


def body(audio, weight, head_weight, clip_owner, node_ids, *, nd, nl):
    nx = math.isqrt(nd)
    ny = nd // nx
    clips, length, chan = audio.shape
    nodes = head_weight.shape[0]
    routes = clip_owner.shape[1]
    pairs = node_ids.shape[2]
    cap = 2 * clips * routes // nl
    slots = nl * cap
    half = chan // 2
    rows_dp, cols_leaf = chan // nd, chan // nl
    span = nodes // nd
    filled = -(-6 * rows_dp // 128) * 128
    chunk = 48
    groups = 4 if nl >= 8 else 2
    steps = clips // chunk
    a = jnp.transpose(audio, (1, 0, 2)).reshape(length // 3, 3, clips, chan)
    w = weight.reshape(2, 3 * chan, chan)
    own = jnp.transpose(clip_owner, (1, 0))
    ids = jnp.transpose(node_ids, (1, 2, 0))
    vm = pltpu.VMEM
    dma = pltpu.SemaphoreType.DMA
    scratch = [
        vm((9, 3, clips, chan), BF16),
        vm((2, 3 * chan, chan), BF16),
        vm((nodes, chan), BF16),
        vm((chan, nodes), BF16),
        vm((9, chunk, chan), F32),
        vm((9, chunk, chan), F32),
        vm((9, clips, chan), BF16),
        vm((9, clips, chan), F32),
        vm((3, clips, chan), F32),
        vm((clips, chan), BF16),
        vm((slots, clips), BF16),
        vm((nl, 2 * pairs, 128), BF16),
        vm((nl, 2 * pairs, 128), BF16),
        vm((slots, chan), BF16),
        vm((slots, chan), BF16),
        vm((slots, nodes), BF16),
        vm((slots, nodes), BF16),
        vm((slots, nodes), BF16),
        vm((slots, chan), BF16),
        vm((slots, chan), BF16),
        vm((ny, nx, span, chan), BF16),
        vm((2, ny - 1, ny, span // 2, chan), BF16),
        vm((2, ny, span // 2, chan), BF16),
        vm((2, ny - 1, span // 2, chan), BF16),
        vm((3, clips, chan), BF16),
        vm((9, clips, chan), BF16),
        vm((6, chan, half), F32),
        vm((6, chan, half), BF16),
        vm((6, chan, half), BF16),
        vm((6, ny, nx, rows_dp, half), BF16),
        vm((6, 2, ny - 1, ny, rows_dp // 2, half), BF16),
        vm((6, 2, ny, rows_dp // 2, half), BF16),
        vm((6, 2, ny - 1, rows_dp // 2, half), BF16),
        vm((filled, half), F32),
        vm((nl // 2, cols_leaf, filled), BF16),
        vm((nl // 2, cols_leaf, filled), BF16),
        vm((max(128, cols_leaf), filled), F32),
        dma((3,)), dma((steps,)), dma((2,)), dma((1,)), dma((nl,)), dma((2,)), dma((4, 2)),
        dma((6,)), dma((6,)), dma((6, 4, 2)), dma((nl // 2,)), dma((nl // 2,)),
    ]
    whole = pl.BlockSpec(memory_space=pltpu.VMEM)
    far = pl.BlockSpec(memory_space=pl.ANY)
    return pl.pallas_call(
        functools.partial(kernel, ny, nx, nl, chunk, groups),
        out_shape=(
            jax.ShapeDtypeStruct((2, 3, rows_dp, cols_leaf), BF16),
            jax.ShapeDtypeStruct((nodes // nd, chan), BF16),
        ),
        in_specs=[far, far, far, whole, whole],
        out_specs=(whole, whole),
        scratch_shapes=scratch,
        compiler_params=pltpu.CompilerParams(
            collective_id=0, has_side_effects=True, vmem_limit_bytes=62914560
        ),
    )(a, w, head_weight, own, ids)


def solution(mesh):
    placed = (
        P(("dp", "leaf"), None, None),
        P(),
        P("leaf", None),
        P(("dp", "leaf"), None),
        P(("dp", "leaf"), None, None),
    )
    return jax.shard_map(
        functools.partial(body, nd=mesh.shape["dp"], nl=mesh.shape["leaf"]),
        mesh=mesh,
        in_specs=placed,
        out_specs=(P(None, None, "dp", "leaf"), P(("leaf", "dp"), None)),
        check_vma=False,
    )
```

```python
import functools
import math

import jax
import jax.numpy as jnp
from jax import lax
from jax.experimental import pallas as pl
from jax.experimental.pallas import tpu as pltpu
from jax.sharding import PartitionSpec as P

MESH = pl.DeviceIdType.MESH
F32 = jnp.float32
BF16 = jnp.bfloat16
INV_ROOT_TWO = 0.7071067811865476
INV_ROOT_TWO_PI = 0.3989422804014327

NT = (((1,), (1,)), ((), ()))
TN = (((0,), (0,)), ((), ()))


def dot(a, b, dims=(((1,), (0,)), ((), ()))):
    return lax.dot_general(a, b, dims, preferred_element_type=F32)


def gelu_pair(value):
    half = 0.5 * (1.0 + lax.erf(value * INV_ROOT_TWO))
    bell = jnp.exp(-0.5 * value * value) * INV_ROOT_TWO_PI
    return value * half, half + value * bell


def bytes_wait(ref, sem):
    pltpu.make_async_copy(ref, ref, sem).wait()


def kernel(
    ny, nx, nl, chunk,
    a_hbm, w_hbm, h_hbm, own_ref, node_ref,
    conv_ref, head_ref,
    a_v, w_v, h_v, ht_v, pa_v, pb_v, a1_v, sl0_v, sl1_v, emb_v, d_v,
    nsend_v, nrecv_v, esend_v, erecv_v, call_v, cpos_v, st_v, gsend_v, grecv_v,
    hsend_v, hone_v, hmid_v, htwo_v, u1_v, u0_v, wown_v, wsend_v, wrecv_v,
    dsend_v, done_v, dmid_v, dtwo_v,
    g_v, zsend_v, zrecv_v, zsum_v,
    load_sem, a_sem, n_sem, e_sem, erecv_sem, g_sem, h_sem, csend_sem, crecv_sem,
    d_sem, zsend_sem, zrecv_sem,
):
    me = lax.axis_index("leaf")
    mine = lax.axis_index("dp")
    core = lax.rem(me, 2)
    sibling = me + 1 - 2 * core
    clips = emb_v.shape[0]
    chan = emb_v.shape[1]
    cap = esend_v.shape[0] // nl
    slots = nl * cap
    nodes = h_v.shape[0]
    pairs = node_ref.shape[1]
    nd = ny * nx
    my_y, my_x = mine // nx, lax.rem(mine, nx)
    half = chan // 2
    span = nodes // nd
    rows_dp = chan // nd
    cols_leaf = chan // nl
    steps = clips // chunk

    load_w0 = pltpu.make_async_copy(w_hbm.at[0], w_v.at[0], load_sem.at[0])
    load_w1 = pltpu.make_async_copy(w_hbm.at[1], w_v.at[1], load_sem.at[1])
    load_h = pltpu.make_async_copy(h_hbm, h_v, load_sem.at[2])

    def load_a(i):
        part = pl.ds(pl.multiple_of(i * chunk, chunk), chunk)
        return pltpu.make_async_copy(a_hbm.at[:, :, part], a_v.at[:, :, part], a_sem.at[i])

    load_w0.start()
    for i in range(steps):
        load_a(i).start()
    load_w1.start()
    load_h.start()

    barrier = pltpu.get_barrier_semaphore()

    @pl.loop(1, nl)
    def _(i):
        pl.semaphore_signal(
            barrier, inc=1, device_id={"leaf": lax.rem(me + i, nl)}, device_id_type=MESH
        )

    @pl.loop(1, nd)
    def _(i):
        pl.semaphore_signal(
            barrier, inc=1, device_id={"dp": lax.rem(mine + i, nd)}, device_id_type=MESH
        )

    owner_iota = lax.broadcasted_iota(jnp.int32, (nl, clips), 0)
    before = (
        lax.broadcasted_iota(jnp.int32, (clips, clips), 0)
        < lax.broadcasted_iota(jnp.int32, (clips, clips), 1)
    ).astype(F32).astype(BF16)
    slot_iota = lax.broadcasted_iota(jnp.int32, (slots, clips), 0)
    list_iota = lax.broadcasted_iota(jnp.int32, (nl * 128, clips), 0)
    base = jnp.zeros((nl, 1), F32)
    spots = []
    lists = jnp.zeros((2 * pairs, nl * 128), F32)
    for r in range(2):
        hit = (own_ref[r : r + 1, :] == owner_iota).astype(F32)
        rank = dot(hit.astype(BF16), before) + base
        base = base + jnp.sum(hit, axis=1, keepdims=True)

        def place(stride):
            spot = jnp.sum(
                hit * (rank + (owner_iota * stride).astype(F32)), axis=0, keepdims=True
            )
            return spot.astype(jnp.int32)

        spots.append((slot_iota == place(cap)).astype(F32).astype(BF16))
        wide = (list_iota == place(128)).astype(F32).astype(BF16)
        ident = node_ref[r] + 1
        parts = jnp.concatenate([ident >> 7, ident & 127], axis=0).astype(F32).astype(BF16)
        lists = lists + dot(parts, wide, NT)
    d_v[...] = spots[0] + spots[1]
    for o in range(nl):
        nsend_v[o] = lists[:, o * 128 : (o + 1) * 128].astype(BF16)

    def block(i):
        return pl.ds(pl.multiple_of(i * cap, cap), cap)

    nz = nl // 2
    my_z = me // 2
    order = []
    for d in range(nz // 2 - 1, 0, -1):
        order.append((d, nz - d))
    order.insert(min(1, len(order)), (nz // 2, 0))
    order = [rel for pair in order for rel in pair]
    per = 4

    def leaf_at(rel, c):
        return 2 * lax.rem(my_z + rel, nz) + c

    def turn(rel):
        return order.index(rel % nz)

    def away():
        for rel in order:
            for c in range(2) if rel else (1 - core,):
                yield leaf_at(rel, c), 2 * turn(rel) + c, 2 * turn(-rel) + core

    home = 2 * turn(0) + core

    load_w0.wait()

    stage = [pa_v, pb_v]

    def multiply(i):
        load_a(i).wait()
        part = pl.ds(i * chunk, chunk)
        folded = jnp.concatenate(
            [a_v[:, k, part, :].reshape(9 * chunk, chan) for k in range(3)], axis=1
        )
        stage[i % 2][...] = dot(folded, w_v[0]).reshape(9, chunk, chan)

    def activate(i):
        part = pl.ds(i * chunk, chunk)

        @pl.loop(0, 9, unroll=True)
        def _(j):
            act, slope = gelu_pair(stage[i % 2][j])
            a1_v[j, part, :] = act.astype(BF16)
            sl0_v[j, part, :] = slope

    multiply(0)
    for i in range(steps):
        if i + 1 < steps:
            multiply(i + 1)
        activate(i)

    load_w1.wait()

    for side in range(2):
        cols = pl.ds(side * half, half)
        for j in range(3):
            folded = jnp.concatenate([a1_v[3 * j + k] for k in range(3)], axis=1)
            sl1_v[j, :, cols] = dot(folded, w_v[1, :, cols])

        @pl.loop(0, steps)
        def _(i):
            part = pl.ds(pl.multiple_of(i * chunk, chunk), chunk)
            total = jnp.zeros((chunk, half), F32)
            for j in range(3):
                act, slope = gelu_pair(sl1_v[j, part, cols])
                sl1_v[j, part, cols] = slope
                total = total + act
            emb_v[part, cols] = (total * (1.0 / 3.0)).astype(BF16)

        esend_v[:, cols] = dot(d_v[...], emb_v[:, cols]).astype(BF16)
        if side == 0:
            pl.semaphore_wait(barrier, nl - 1 + nd - 1)
            nrecv_v[home] = nsend_v[me]
            for to, _, mark in away():
                pltpu.make_async_remote_copy(
                    nsend_v.at[to], nrecv_v.at[mark], n_sem.at[0], n_sem.at[1],
                    device_id={"leaf": to}, device_id_type=MESH,
                ).start()
        for to, _, mark in away():
            pltpu.make_async_remote_copy(
                esend_v.at[block(to), cols], erecv_v.at[block(mark), cols], e_sem.at[0],
                erecv_sem.at[mark], device_id={"leaf": to}, device_id_type=MESH,
            ).start()
    erecv_v[block(home), :] = esend_v[block(me), :]

    load_h.wait()
    piece = nodes // 4

    for i in range(4):
        ht_v[:, i * piece : (i + 1) * piece] = h_v[i * piece : (i + 1) * piece, :].T

    bytes_wait(nsend_v.at[pl.ds(0, nl - 1)], n_sem.at[0])
    bytes_wait(nrecv_v.at[pl.ds(0, nl - 1)], n_sem.at[1])
    node_iota = lax.broadcasted_iota(jnp.int32, (16, nodes), 1).astype(F32)

    @pl.loop(0, nl)
    def _(o):
        parts = nrecv_v[o].astype(F32)
        named = (parts[:pairs] * 128.0 + parts[pairs:] - 1.0).T
        for i in range(cap // 16):
            part = pl.ds(pl.multiple_of(o * cap + i * 16, 16), 16)
            tally = jnp.zeros((16, nodes), F32)
            for q in range(pairs):
                weight = 17.0 if q < pairs // 2 else 1.0
                ident = named[i * 16 : (i + 1) * 16, q : q + 1]
                tally = tally + jnp.where(ident == node_iota, weight, 0.0)
            positive = jnp.floor(tally * (1.0 / 16.0))
            cpos_v[part, :] = positive.astype(BF16)
            call_v[part, :] = (tally - 16.0 * positive).astype(BF16)

    lanes = nodes // 4
    for t in range(nl // per):
        sources = []
        for rel in order[2 * t : 2 * t + 2]:
            for c in range(2) if rel else (1 - core,):
                sources.append((leaf_at(rel, c), 2 * turn(rel) + c))
        for _, place in sources:
            bytes_wait(erecv_v.at[block(place)], erecv_sem.at[place])
        rows = pl.ds(t * per * cap, per * cap)
        emb = erecv_v[rows, :]

        @pl.loop(0, 4)
        def _(n):
            cols = pl.ds(pl.multiple_of(n * lanes, lanes), lanes)
            score = dot(emb, ht_v[:, cols])
            sig = 0.5 * jnp.tanh(0.5 * score) + 0.5
            st_v[rows, cols] = (
                sig * call_v[rows, cols].astype(F32) - cpos_v[rows, cols].astype(F32)
            ).astype(BF16)

        gsend_v[rows, :] = dot(st_v[rows, :], h_v[...]).astype(BF16)
        if 0 in order[2 * t : 2 * t + 2]:
            grecv_v[block(me), :] = gsend_v[block(home), :]
        for to, place in sources:
            pltpu.make_async_remote_copy(
                gsend_v.at[block(place)], grecv_v.at[block(me)], g_sem.at[0], g_sem.at[1],
                device_id={"leaf": to}, device_id_type=MESH,
            ).start()

    low_rows, high_rows = pl.ds(0, span // 2), pl.ds(span // 2, span // 2)

    def over_x(o):
        return {"dp": my_y * nx + lax.rem(my_x + o, nx)}

    def over_y(o):
        return {"dp": lax.rem(my_y + o, ny) * nx + my_x}

    def send(source, target, sems, device):
        pltpu.make_async_remote_copy(
            source, target, sems.at[0], sems.at[1], device_id=device, device_id_type=MESH
        ).start()

    for o in range(1, ny + 1):
        y = lax.rem(my_y + o, ny)
        cols = pl.ds(pl.multiple_of(y * nx * span, nx * span), nx * span)
        terms = dot(st_v[:, cols], erecv_v[...], TN).astype(BF16)
        hsend_v[y] = terms.reshape(nx, span, chan)
        if o < ny:
            send(hsend_v.at[y, :, high_rows], hone_v.at[1, o - 1], h_sem.at[1], over_y(o))
    for o in range(1, nx):
        x = lax.rem(my_x + o, nx)
        send(hsend_v.at[:, x, low_rows], hone_v.at[0, o - 1], h_sem.at[0], over_x(o))

    bytes_wait(hone_v.at[1], h_sem.at[1, 1])
    bytes_wait(hone_v.at[0], h_sem.at[0, 1])
    strip = 32

    @pl.loop(0, ny)
    def _(i):
        for at in range(0, span // 2, strip):
            part = pl.ds(at, strip)
            total = hsend_v[i, my_x, part, :].astype(F32)
            for o in range(nx - 1):
                total = total + hone_v[0, o, i, part, :].astype(F32)
            hmid_v[0, i, part, :] = total.astype(BF16)
            total = hsend_v[my_y, i, pl.ds(span // 2 + at, strip), :].astype(F32)
            for o in range(ny - 1):
                total = total + hone_v[1, o, i, part, :].astype(F32)
            hmid_v[1, i, part, :] = total.astype(BF16)

    for o in range(1, ny):
        send(hmid_v.at[0, lax.rem(my_y + o, ny)], htwo_v.at[0, o - 1], h_sem.at[2], over_y(o))
        send(hmid_v.at[1, lax.rem(my_x + o, nx)], htwo_v.at[1, o - 1], h_sem.at[3], over_x(o))

    bytes_wait(grecv_v.at[pl.ds(0, (nl - 1) * cap)], g_sem.at[1])
    clip_grad = dot(d_v[...], grecv_v[...], TN) * (1.0 / 3.0)
    for j in range(3):
        u1_v[j] = (clip_grad * sl1_v[j]).astype(BF16)

    def leave(step, grad):
        low, high = grad[:, :half], grad[:, half:]
        wown_v[step] = jnp.where(core == 0, low, high)
        wsend_v[step] = jnp.where(core == 0, high, low).astype(BF16)
        core_copy(step).start()

    def core_copy(step):
        return pltpu.make_async_remote_copy(
            wsend_v.at[step], wrecv_v.at[step], csend_sem.at[step], crecv_sem.at[step],
            device_id={"leaf": sibling}, device_id_type=MESH,
        )

    part_rows = rows_dp // 2
    low_part, high_part = pl.ds(0, part_rows), pl.ds(part_rows, part_rows)

    def spread(step):
        core_copy(step).wait_recv()
        both = (wown_v[step] + wrecv_v[step].astype(F32)).astype(BF16)
        dsend_v[step] = both.reshape(ny, nx, rows_dp, half)
        for o in range(1, nx):
            x = lax.rem(my_x + o, nx)
            send(
                dsend_v.at[step, :, x, low_part], done_v.at[step, 0, o - 1],
                d_sem.at[step, 0], over_x(o),
            )
        for o in range(1, ny):
            y = lax.rem(my_y + o, ny)
            send(
                dsend_v.at[step, y, :, high_part], done_v.at[step, 1, o - 1],
                d_sem.at[step, 1], over_y(o),
            )

    def respread(step):
        bytes_wait(done_v.at[step, 0], d_sem.at[step, 0, 1])
        total = dsend_v[step, :, my_x, low_part, :].astype(F32)
        for o in range(nx - 1):
            total = total + done_v[step, 0, o].astype(F32)
        dmid_v[step, 0] = total.astype(BF16)
        bytes_wait(done_v.at[step, 1], d_sem.at[step, 1, 1])
        total = dsend_v[step, my_y, :, high_part, :].astype(F32)
        for o in range(ny - 1):
            total = total + done_v[step, 1, o].astype(F32)
        dmid_v[step, 1] = total.astype(BF16)
        for o in range(1, ny):
            send(
                dmid_v.at[step, 0, lax.rem(my_y + o, ny)], dtwo_v.at[step, 0, o - 1],
                d_sem.at[step, 2], over_y(o),
            )
            send(
                dmid_v.at[step, 1, lax.rem(my_x + o, nx)], dtwo_v.at[step, 1, o - 1],
                d_sem.at[step, 3], over_x(o),
            )

    def gather_step(step):
        for side, place in ((0, my_y), (1, my_x)):
            bytes_wait(dtwo_v.at[step, side], d_sem.at[step, 2 + side, 1])
            total = dmid_v[step, side, place].astype(F32)
            for o in range(ny - 1):
                total = total + dtwo_v[step, side, o].astype(F32)
            first = pl.multiple_of(step * rows_dp + side * part_rows, part_rows)
            g_v[pl.ds(first, part_rows), :] = total

    @pl.loop(0, 3)
    def _(k):
        left = jnp.concatenate([a1_v[3 * j + k] for j in range(3)], axis=0)
        leave(3 + k, dot(left, u1_v[...].reshape(3 * clips, chan), TN))

    @pl.loop(0, 3)
    def _(k):
        taps = w_v[1, pl.ds(pl.multiple_of(k * chan, chan), chan), :]
        for j in range(3):
            u0_v[3 * j + k] = (dot(u1_v[j], taps, NT) * sl0_v[3 * j + k]).astype(BF16)

    @pl.loop(0, 3)
    def _(k):
        spread(3 + k)

    @pl.loop(0, 3)
    def _(k):
        left = a_v[:, k].reshape(9 * clips, chan)
        leave(k, dot(left, u0_v[...].reshape(9 * clips, chan), TN))

        @pl.when(k > 0)
        def _():
            spread(k - 1)

    spread(2)

    filled = 6 * rows_dp
    if g_v.shape[0] > filled:
        g_v[filled:, :] = jnp.zeros((g_v.shape[0] - filled, half), F32)

    @pl.loop(0, 3)
    def _(k):
        respread(3 + k)

    @pl.loop(0, 3)
    def _(k):
        respread(k)

    for side, place in ((0, my_y), (1, my_x)):
        bytes_wait(htwo_v.at[side], h_sem.at[2 + side, 1])
        for at in range(0, span // 2, strip):
            part = pl.ds(at, strip)
            total = hmid_v[side, place, part, :].astype(F32)
            for o in range(ny - 1):
                total = total + htwo_v[side, o, part, :].astype(F32)
            head_ref[pl.ds(side * (span // 2) + at, strip), :] = total.astype(BF16)

    @pl.loop(0, 3)
    def _(k):
        gather_step(3 + k)

    @pl.loop(0, 3)
    def _(k):
        gather_step(k)

    zsend_v[...] = g_v[...].T.astype(BF16).reshape(nl // 2, cols_leaf, g_v.shape[0])
    for i in range(nl // 2):
        to = core * (nl // 2) + i

        @pl.when(to == me)
        def _():
            zrecv_v[my_z] = zsend_v[i]

        @pl.when(to != me)
        def _():
            pltpu.make_async_remote_copy(
                zsend_v.at[i], zrecv_v.at[my_z], zsend_sem.at[i], zrecv_sem.at[my_z],
                device_id={"leaf": to}, device_id_type=MESH,
            ).start()

    giver = me // (nl // 2)
    zsum_v[...] = jnp.zeros(zsum_v.shape, F32)
    for z in range(nl // 2):

        @pl.when(2 * z + giver != me)
        def _():
            pltpu.make_async_remote_copy(
                zsend_v.at[z], zrecv_v.at[z], zsend_sem.at[z], zrecv_sem.at[z],
                device_id={"leaf": sibling}, device_id_type=MESH,
            ).wait_recv()

    total = zrecv_v[0].astype(F32)
    for z in range(1, nl // 2):
        total = total + zrecv_v[z].astype(F32)
    zsum_v[0:cols_leaf, :] = total
    final = zsum_v[...].T[:filled, :cols_leaf]
    conv_ref[...] = final.reshape(2, 3, rows_dp, cols_leaf).astype(BF16)

    bytes_wait(esend_v.at[pl.ds(0, (nl - 1) * cap)], e_sem.at[0])
    bytes_wait(gsend_v.at[pl.ds(0, (nl - 1) * cap)], g_sem.at[0])
    for side in range(2):
        bytes_wait(hone_v.at[side], h_sem.at[side, 0])
        bytes_wait(htwo_v.at[side], h_sem.at[2 + side, 0])

    @pl.loop(0, 6)
    def _(step):
        core_copy(step).wait_send()
        for side in range(2):
            bytes_wait(done_v.at[step, side], d_sem.at[step, side, 0])
            bytes_wait(dtwo_v.at[step, side], d_sem.at[step, 2 + side, 0])

    for i in range(nl // 2):

        @pl.when(core * (nl // 2) + i != me)
        def _():
            pltpu.make_async_remote_copy(
                zsend_v.at[i], zrecv_v.at[my_z], zsend_sem.at[i], zrecv_sem.at[my_z],
                device_id={"leaf": sibling}, device_id_type=MESH,
            ).wait_send()


def hand_on(conv_ref, head_ref, conv_out, head_out):
    conv_out[...] = conv_ref[...]
    head_out[...] = head_ref[...]


def body(audio, weight, head_weight, clip_owner, node_ids, *, nd, nl):
    nx = math.isqrt(nd)
    ny = nd // nx
    clips, length, chan = audio.shape
    nodes = head_weight.shape[0]
    routes = clip_owner.shape[1]
    pairs = node_ids.shape[2]
    cap = 2 * clips * routes // nl
    slots = nl * cap
    half = chan // 2
    rows_dp, cols_leaf = chan // nd, chan // nl
    span = nodes // nd
    filled = -(-6 * rows_dp // 128) * 128
    chunk = 48
    steps = clips // chunk
    a = jnp.transpose(audio, (1, 0, 2)).reshape(length // 3, 3, clips, chan)
    w = weight.reshape(2, 3 * chan, chan)
    own = jnp.transpose(clip_owner, (1, 0))
    ids = jnp.transpose(node_ids, (1, 2, 0))
    vm = pltpu.VMEM
    dma = pltpu.SemaphoreType.DMA
    scratch = [
        vm((9, 3, clips, chan), BF16),
        vm((2, 3 * chan, chan), BF16),
        vm((nodes, chan), BF16),
        vm((chan, nodes), BF16),
        vm((9, chunk, chan), F32),
        vm((9, chunk, chan), F32),
        vm((9, clips, chan), BF16),
        vm((9, clips, chan), F32),
        vm((3, clips, chan), F32),
        vm((clips, chan), BF16),
        vm((slots, clips), BF16),
        vm((nl, 2 * pairs, 128), BF16),
        vm((nl, 2 * pairs, 128), BF16),
        vm((slots, chan), BF16),
        vm((slots, chan), BF16),
        vm((slots, nodes), BF16),
        vm((slots, nodes), BF16),
        vm((slots, nodes), BF16),
        vm((slots, chan), BF16),
        vm((slots, chan), BF16),
        vm((ny, nx, span, chan), BF16),
        vm((2, ny - 1, ny, span // 2, chan), BF16),
        vm((2, ny, span // 2, chan), BF16),
        vm((2, ny - 1, span // 2, chan), BF16),
        vm((3, clips, chan), BF16),
        vm((9, clips, chan), BF16),
        vm((6, chan, half), F32),
        vm((6, chan, half), BF16),
        vm((6, chan, half), BF16),
        vm((6, ny, nx, rows_dp, half), BF16),
        vm((6, 2, ny - 1, ny, rows_dp // 2, half), BF16),
        vm((6, 2, ny, rows_dp // 2, half), BF16),
        vm((6, 2, ny - 1, rows_dp // 2, half), BF16),
        vm((filled, half), F32),
        vm((nl // 2, cols_leaf, filled), BF16),
        vm((nl // 2, cols_leaf, filled), BF16),
        vm((max(128, cols_leaf), filled), F32),
        dma((3,)), dma((steps,)), dma((2,)), dma((1,)), dma((nl,)), dma((2,)), dma((4, 2)),
        dma((6,)), dma((6,)), dma((6, 4, 2)), dma((nl // 2,)), dma((nl // 2,)),
    ]
    whole = pl.BlockSpec(memory_space=pltpu.VMEM)
    far = pl.BlockSpec(memory_space=pl.ANY)
    conv, head = pl.pallas_call(
        functools.partial(kernel, ny, nx, nl, chunk),
        out_shape=(
            jax.ShapeDtypeStruct((2, 3, rows_dp, cols_leaf), BF16),
            jax.ShapeDtypeStruct((nodes // nd, chan), BF16),
        ),
        in_specs=[far, far, far, whole, whole],
        out_specs=(whole, whole),
        scratch_shapes=scratch,
        compiler_params=pltpu.CompilerParams(
            collective_id=0, has_side_effects=True, vmem_limit_bytes=62914560
        ),
    )(a, w, head_weight, own, ids)
    return pl.pallas_call(
        hand_on,
        out_shape=(
            jax.ShapeDtypeStruct(conv.shape, BF16),
            jax.ShapeDtypeStruct(head.shape, BF16),
        ),
        in_specs=[whole, whole],
        out_specs=(whole, whole),
    )(conv, head)


def solution(mesh):
    placed = (
        P(("dp", "leaf"), None, None),
        P(),
        P("leaf", None),
        P(("dp", "leaf"), None),
        P(("dp", "leaf"), None, None),
    )
    return jax.shard_map(
        functools.partial(body, nd=mesh.shape["dp"], nl=mesh.shape["leaf"]),
        mesh=mesh,
        in_specs=placed,
        out_specs=(P(None, None, "dp", "leaf"), P(("leaf", "dp"), None)),
        check_vma=False,
    )
```

```python
import functools
import math

import jax
import jax.numpy as jnp
from jax import lax
from jax.experimental import pallas as pl
from jax.experimental.pallas import tpu as pltpu
from jax.sharding import PartitionSpec as P

MESH = pl.DeviceIdType.MESH
F32 = jnp.float32
BF16 = jnp.bfloat16
INV_ROOT_TWO = 0.7071067811865476
INV_ROOT_TWO_PI = 0.3989422804014327

NT = (((1,), (1,)), ((), ()))
TN = (((0,), (0,)), ((), ()))


def dot(a, b, dims=(((1,), (0,)), ((), ()))):
    return lax.dot_general(a, b, dims, preferred_element_type=F32)


def gelu_pair(value):
    half = 0.5 * (1.0 + lax.erf(value * INV_ROOT_TWO))
    bell = jnp.exp(-0.5 * value * value) * INV_ROOT_TWO_PI
    return value * half, half + value * bell


def bytes_wait(ref, sem):
    pltpu.make_async_copy(ref, ref, sem).wait()


def kernel(
    ny, nx, nl, chunk,
    a_hbm, w_hbm, h_hbm, own_ref, node_ref,
    conv_ref, head_ref,
    a_v, w_v, h_v, ht_v, pa_v, pb_v, a1_v, sl0_v, sl1_v, emb_v, d_v,
    nsend_v, nrecv_v, esend_v, erecv_v, call_v, cpos_v, st_v, gsend_v, grecv_v,
    hsend_v, hfar_v, hnear_v, hsum_v, hgot_v, hmid_v, htwo_v, u1_v, u0_v, wown_v, wsend_v, wrecv_v,
    dsend_v, dfar_v, dnear_v, dsum_v, dgot_v, dmid_v, dtwo_v,
    g_v, zsend_v, zrecv_v, zsum_v,
    load_sem, a_sem, n_sem, e_sem, erecv_sem, g_sem, h_sem, csend_sem, crecv_sem,
    d_sem, zsend_sem, zrecv_sem,
):
    me = lax.axis_index("leaf")
    mine = lax.axis_index("dp")
    core = lax.rem(me, 2)
    sibling = me + 1 - 2 * core
    clips = emb_v.shape[0]
    chan = emb_v.shape[1]
    cap = esend_v.shape[0] // nl
    slots = nl * cap
    nodes = h_v.shape[0]
    pairs = node_ref.shape[1]
    nd = ny * nx
    my_y, my_x = mine // nx, lax.rem(mine, nx)
    half = chan // 2
    span = nodes // nd
    rows_dp = chan // nd
    cols_leaf = chan // nl
    steps = clips // chunk

    load_w0 = pltpu.make_async_copy(w_hbm.at[0], w_v.at[0], load_sem.at[0])
    load_w1 = pltpu.make_async_copy(w_hbm.at[1], w_v.at[1], load_sem.at[1])
    load_h = pltpu.make_async_copy(h_hbm, h_v, load_sem.at[2])

    def load_a(i):
        part = pl.ds(pl.multiple_of(i * chunk, chunk), chunk)
        return pltpu.make_async_copy(a_hbm.at[:, :, part], a_v.at[:, :, part], a_sem.at[i])

    load_w0.start()
    for i in range(steps):
        load_a(i).start()
    load_w1.start()
    load_h.start()

    barrier = pltpu.get_barrier_semaphore()

    @pl.loop(1, nl)
    def _(i):
        pl.semaphore_signal(
            barrier, inc=1, device_id={"leaf": lax.rem(me + i, nl)}, device_id_type=MESH
        )

    @pl.loop(1, nd)
    def _(i):
        pl.semaphore_signal(
            barrier, inc=1, device_id={"dp": lax.rem(mine + i, nd)}, device_id_type=MESH
        )

    owner_iota = lax.broadcasted_iota(jnp.int32, (nl, clips), 0)
    before = (
        lax.broadcasted_iota(jnp.int32, (clips, clips), 0)
        < lax.broadcasted_iota(jnp.int32, (clips, clips), 1)
    ).astype(F32).astype(BF16)
    slot_iota = lax.broadcasted_iota(jnp.int32, (slots, clips), 0)
    list_iota = lax.broadcasted_iota(jnp.int32, (nl * 128, clips), 0)
    base = jnp.zeros((nl, 1), F32)
    spots = []
    lists = jnp.zeros((2 * pairs, nl * 128), F32)
    for r in range(2):
        hit = (own_ref[r : r + 1, :] == owner_iota).astype(F32)
        rank = dot(hit.astype(BF16), before) + base
        base = base + jnp.sum(hit, axis=1, keepdims=True)

        def place(stride):
            spot = jnp.sum(
                hit * (rank + (owner_iota * stride).astype(F32)), axis=0, keepdims=True
            )
            return spot.astype(jnp.int32)

        spots.append((slot_iota == place(cap)).astype(F32).astype(BF16))
        wide = (list_iota == place(128)).astype(F32).astype(BF16)
        ident = node_ref[r] + 1
        parts = jnp.concatenate([ident >> 7, ident & 127], axis=0).astype(F32).astype(BF16)
        lists = lists + dot(parts, wide, NT)
    d_v[...] = spots[0] + spots[1]
    for o in range(nl):
        nsend_v[o] = lists[:, o * 128 : (o + 1) * 128].astype(BF16)

    def block(i):
        return pl.ds(pl.multiple_of(i * cap, cap), cap)

    nz = nl // 2
    my_z = me // 2
    order = []
    for d in range(nz // 2 - 1, 0, -1):
        order.append((d, nz - d))
    order.insert(min(1, len(order)), (nz // 2, 0))
    order = [rel for pair in order for rel in pair]
    per = 4

    def leaf_at(rel, c):
        return 2 * lax.rem(my_z + rel, nz) + c

    def turn(rel):
        return order.index(rel % nz)

    def away():
        for rel in order:
            for c in range(2) if rel else (1 - core,):
                yield leaf_at(rel, c), 2 * turn(rel) + c, 2 * turn(-rel) + core

    home = 2 * turn(0) + core

    load_w0.wait()

    stage = [pa_v, pb_v]

    def multiply(i):
        load_a(i).wait()
        part = pl.ds(i * chunk, chunk)
        folded = jnp.concatenate(
            [a_v[:, k, part, :].reshape(9 * chunk, chan) for k in range(3)], axis=1
        )
        stage[i % 2][...] = dot(folded, w_v[0]).reshape(9, chunk, chan)

    def activate(i):
        part = pl.ds(i * chunk, chunk)

        @pl.loop(0, 9, unroll=True)
        def _(j):
            act, slope = gelu_pair(stage[i % 2][j])
            a1_v[j, part, :] = act.astype(BF16)
            sl0_v[j, part, :] = slope

    multiply(0)
    for i in range(steps):
        if i + 1 < steps:
            multiply(i + 1)
        activate(i)

    load_w1.wait()

    for side in range(2):
        cols = pl.ds(side * half, half)
        for j in range(3):
            folded = jnp.concatenate([a1_v[3 * j + k] for k in range(3)], axis=1)
            sl1_v[j, :, cols] = dot(folded, w_v[1, :, cols])

        @pl.loop(0, steps, unroll=True)
        def _(i):
            part = pl.ds(pl.multiple_of(i * chunk, chunk), chunk)
            total = jnp.zeros((chunk, half), F32)
            for j in range(3):
                act, slope = gelu_pair(sl1_v[j, part, cols])
                sl1_v[j, part, cols] = slope
                total = total + act
            emb_v[part, cols] = (total * (1.0 / 3.0)).astype(BF16)

        esend_v[:, cols] = dot(d_v[...], emb_v[:, cols]).astype(BF16)
        if side == 0:
            pl.semaphore_wait(barrier, nl - 1 + nd - 1)
            nrecv_v[home] = nsend_v[me]
            for to, _, mark in away():
                pltpu.make_async_remote_copy(
                    nsend_v.at[to], nrecv_v.at[mark], n_sem.at[0], n_sem.at[1],
                    device_id={"leaf": to}, device_id_type=MESH,
                ).start()
        for to, _, mark in away():
            pltpu.make_async_remote_copy(
                esend_v.at[block(to), cols], erecv_v.at[block(mark), cols], e_sem.at[0],
                erecv_sem.at[mark], device_id={"leaf": to}, device_id_type=MESH,
            ).start()
    erecv_v[block(home), :] = esend_v[block(me), :]

    load_h.wait()
    piece = nodes // 4

    for i in range(4):
        ht_v[:, i * piece : (i + 1) * piece] = h_v[i * piece : (i + 1) * piece, :].T

    bytes_wait(nsend_v.at[pl.ds(0, nl - 1)], n_sem.at[0])
    bytes_wait(nrecv_v.at[pl.ds(0, nl - 1)], n_sem.at[1])
    node_iota = lax.broadcasted_iota(jnp.int32, (16, nodes), 1).astype(F32)

    @pl.loop(0, nl)
    def _(o):
        parts = nrecv_v[o].astype(F32)
        named = (parts[:pairs] * 128.0 + parts[pairs:] - 1.0).T
        for i in range(cap // 16):
            part = pl.ds(pl.multiple_of(o * cap + i * 16, 16), 16)
            tally = jnp.zeros((16, nodes), F32)
            for q in range(pairs):
                weight = 17.0 if q < pairs // 2 else 1.0
                ident = named[i * 16 : (i + 1) * 16, q : q + 1]
                tally = tally + jnp.where(ident == node_iota, weight, 0.0)
            positive = jnp.floor(tally * (1.0 / 16.0))
            every = 0.5 * tally - 8.0 * positive
            call_v[part, :] = every.astype(BF16)
            cpos_v[part, :] = (every - positive).astype(BF16)

    lanes = nodes // 4
    for t in range(nl // per):
        sources = []
        for rel in order[2 * t : 2 * t + 2]:
            for c in range(2) if rel else (1 - core,):
                sources.append((leaf_at(rel, c), 2 * turn(rel) + c))
        for _, place in sources:
            bytes_wait(erecv_v.at[block(place)], erecv_sem.at[place])
        rows = pl.ds(t * per * cap, per * cap)
        emb = erecv_v[rows, :]

        for n in range(4):
            cols = pl.ds(n * lanes, lanes)
            score = dot(emb, ht_v[:, cols])
            st_v[rows, cols] = (
                jnp.tanh(0.5 * score) * call_v[rows, cols].astype(F32)
                + cpos_v[rows, cols].astype(F32)
            ).astype(BF16)

        gsend_v[rows, :] = dot(st_v[rows, :], h_v[...]).astype(BF16)
        if 0 in order[2 * t : 2 * t + 2]:
            grecv_v[block(me), :] = gsend_v[block(home), :]
        for to, place in sources:
            pltpu.make_async_remote_copy(
                gsend_v.at[block(place)], grecv_v.at[block(me)], g_sem.at[0], g_sem.at[1],
                device_id={"leaf": to}, device_id_type=MESH,
            ).start()

    low_rows, high_rows = pl.ds(0, span // 2), pl.ds(span // 2, span // 2)

    def over_x(o):
        return {"dp": my_y * nx + lax.rem(my_x + o, nx)}

    def over_y(o):
        return {"dp": lax.rem(my_y + o, ny) * nx + my_x}

    def send(source, target, sems, device):
        pltpu.make_async_remote_copy(
            source, target, sems.at[0], sems.at[1], device_id=device, device_id_type=MESH
        ).start()

    def beside(side, o):
        if side == 0:
            return over_x(o), lax.rem(my_x + o, nx)
        return over_y(o), lax.rem(my_y + o, ny)

    def piece(ref, side, at, rows, cols):
        if side == 0:
            return ref.at[:, at, rows[0], cols]
        return ref.at[at, :, rows[1], cols]

    def halves(width):
        return pl.ds(0, width // 2), pl.ds(width // 2, width // 2)

    def send_far(ref, side, rows, cols, far, sems):
        _, at = beside(side, 2)
        for way, o in ((0, 1), (1, 3)):
            to, _ = beside(side, o)
            send(piece(ref, side, at, rows, cols[way]), far.at[side, way], sems.at[side], to)

    def send_near(ref, side, rows, cols, near, sems, way):
        to, at = beside(side, 1 + 2 * way)
        send(piece(ref, side, at, rows, cols[1 - way]), near.at[side, way], sems.at[2 + side], to)

    def pass_on(ref, rows, cols, far, added, got, sems):
        for side in range(2):
            bytes_wait(far.at[side], sems.at[side, 1])
            for way in range(2):
                to, at = beside(side, 1 + 2 * way)
                own = piece(ref, side, at, rows, cols[way])
                for i in range(ny):
                    added[side, way, i] = (
                        own[i].astype(F32) + far[side, way, i].astype(F32)
                    ).astype(BF16)
                send(added.at[side, way], got.at[side, way], sems.at[4 + side], to)

    def add_up(ref, rows, cols, near, got, middle, two, sems):
        for side in range(2):
            bytes_wait(near.at[side], sems.at[2 + side, 1])
            bytes_wait(got.at[side], sems.at[4 + side, 1])
            _, at = beside(side, 0)
            for way in range(2):
                own = piece(ref, side, at, rows, cols[way])
                for i in range(ny):
                    middle[side, i, :, cols[way]] = (
                        own[i].astype(F32)
                        + got[side, way, i].astype(F32)
                        + near[side, 1 - way, i].astype(F32)
                    ).astype(BF16)
        for side in range(2):
            for o in (2, 1, 3):
                to, at = beside(1 - side, o)
                send(middle.at[side, at], two.at[side, o - 1], sems.at[6 + side], to)

    def drain(far, near, got, two, sems):
        for side in range(2):
            bytes_wait(far.at[side], sems.at[side, 0])
            bytes_wait(near.at[side], sems.at[2 + side, 0])
            bytes_wait(got.at[side], sems.at[4 + side, 0])
            bytes_wait(two.at[side], sems.at[6 + side, 0])

    head_rows = (low_rows, high_rows)
    wide = halves(chan)
    for o in (2, 1, 3, 0):
        y = lax.rem(my_y + o, ny)
        cols = pl.ds(pl.multiple_of(y * nx * span, nx * span), nx * span)
        terms = dot(st_v[:, cols], erecv_v[...], TN).astype(BF16)
        hsend_v[y] = terms.reshape(nx, span, chan)
        if o == 2:
            send_far(hsend_v, 1, head_rows, wide, hfar_v, h_sem)
        elif o:
            send_near(hsend_v, 1, head_rows, wide, hnear_v, h_sem, o // 2)
    send_far(hsend_v, 0, head_rows, wide, hfar_v, h_sem)
    for way in range(2):
        send_near(hsend_v, 0, head_rows, wide, hnear_v, h_sem, way)

    pass_on(hsend_v, head_rows, wide, hfar_v, hsum_v, hgot_v, h_sem)
    strip = 32

    bytes_wait(grecv_v.at[pl.ds(0, (nl - 1) * cap)], g_sem.at[1])
    clip_grad = dot(d_v[...], grecv_v[...], TN) * (1.0 / 3.0)
    for j in range(3):
        u1_v[j] = (clip_grad * sl1_v[j]).astype(BF16)

    def leave(step, grad):
        low, high = grad[:, :half], grad[:, half:]
        wown_v[step] = jnp.where(core == 0, low, high)
        wsend_v[step] = jnp.where(core == 0, high, low).astype(BF16)
        core_copy(step).start()

    def core_copy(step):
        return pltpu.make_async_remote_copy(
            wsend_v.at[step], wrecv_v.at[step], csend_sem.at[step], crecv_sem.at[step],
            device_id={"leaf": sibling}, device_id_type=MESH,
        )

    part_rows = rows_dp // 2
    conv_rows = (pl.ds(0, part_rows), pl.ds(part_rows, part_rows))
    thin = halves(half)

    def spread(step):
        core_copy(step).wait_recv()
        both = (wown_v[step] + wrecv_v[step].astype(F32)).astype(BF16)
        dsend_v[step] = both.reshape(ny, nx, rows_dp, half)
        for side in range(2):
            send_far(dsend_v.at[step], side, conv_rows, thin, dfar_v.at[step], d_sem.at[step])
        for side in range(2):
            for way in range(2):
                send_near(
                    dsend_v.at[step], side, conv_rows, thin, dnear_v.at[step], d_sem.at[step], way
                )

    def carry(step):
        pass_on(
            dsend_v.at[step], conv_rows, thin, dfar_v.at[step], dsum_v.at[step],
            dgot_v.at[step], d_sem.at[step],
        )

    def respread(step):
        add_up(
            dsend_v.at[step], conv_rows, thin, dnear_v.at[step], dgot_v.at[step],
            dmid_v.at[step], dtwo_v.at[step], d_sem.at[step],
        )

    def gather_step(step):
        for side, place in ((0, my_y), (1, my_x)):
            bytes_wait(dtwo_v.at[step, side], d_sem.at[step, 6 + side, 1])
            total = dmid_v[step, side, place].astype(F32)
            for o in range(ny - 1):
                total = total + dtwo_v[step, side, o].astype(F32)
            g_v[pl.ds(step * rows_dp + side * part_rows, part_rows), :] = total

    for k in range(3):
        left = jnp.concatenate([a1_v[3 * j + k] for j in range(3)], axis=0)
        leave(3 + k, dot(left, u1_v[...].reshape(3 * clips, chan), TN))

    for k in range(3):
        taps = w_v[1, k * chan : (k + 1) * chan, :]
        for j in range(3):
            u0_v[3 * j + k] = (dot(u1_v[j], taps, NT) * sl0_v[3 * j + k]).astype(BF16)

    for k in range(3):
        spread(3 + k)

    for k in range(3):
        left = a_v[:, k].reshape(9 * clips, chan)
        leave(k, dot(left, u0_v[...].reshape(9 * clips, chan), TN))
        if k == 0:
            for step in (3, 4, 5):
                carry(step)
            add_up(hsend_v, head_rows, wide, hnear_v, hgot_v, hmid_v, htwo_v, h_sem)
        else:
            spread(k - 1)

    spread(2)
    carry(0)
    carry(1)

    filled = 6 * rows_dp
    if g_v.shape[0] > filled:
        g_v[filled:, :] = jnp.zeros((g_v.shape[0] - filled, half), F32)

    for step in (3, 4, 5):
        respread(step)
    carry(2)
    for step in range(3):
        respread(step)

    for step in (3, 4, 5, 0, 1, 2):
        gather_step(step)

    zsend_v[...] = g_v[...].T.astype(BF16).reshape(nl // 2, cols_leaf, g_v.shape[0])
    for i in range(nl // 2):
        to = core * (nl // 2) + i

        @pl.when(to == me)
        def _():
            zrecv_v[my_z] = zsend_v[i]

        @pl.when(to != me)
        def _():
            pltpu.make_async_remote_copy(
                zsend_v.at[i], zrecv_v.at[my_z], zsend_sem.at[i], zrecv_sem.at[my_z],
                device_id={"leaf": to}, device_id_type=MESH,
            ).start()

    for side, place in ((0, my_y), (1, my_x)):
        bytes_wait(htwo_v.at[side], h_sem.at[6 + side, 1])
        for at in range(0, span // 2, strip):
            part = pl.ds(at, strip)
            total = hmid_v[side, place, part, :].astype(F32)
            for o in range(ny - 1):
                total = total + htwo_v[side, o, part, :].astype(F32)
            head_ref[pl.ds(side * (span // 2) + at, strip), :] = total.astype(BF16)

    giver = me // (nl // 2)
    zsum_v[...] = jnp.zeros(zsum_v.shape, F32)
    for z in range(nl // 2):

        @pl.when(2 * z + giver != me)
        def _():
            pltpu.make_async_remote_copy(
                zsend_v.at[z], zrecv_v.at[z], zsend_sem.at[z], zrecv_sem.at[z],
                device_id={"leaf": sibling}, device_id_type=MESH,
            ).wait_recv()

    total = zrecv_v[0].astype(F32)
    for z in range(1, nl // 2):
        total = total + zrecv_v[z].astype(F32)
    zsum_v[0:cols_leaf, :] = total
    final = zsum_v[...].T[:filled, :cols_leaf]
    conv_ref[...] = final.reshape(2, 3, rows_dp, cols_leaf).astype(BF16)

    bytes_wait(esend_v.at[pl.ds(0, (nl - 1) * cap)], e_sem.at[0])
    bytes_wait(gsend_v.at[pl.ds(0, (nl - 1) * cap)], g_sem.at[0])
    drain(hfar_v, hnear_v, hgot_v, htwo_v, h_sem)

    @pl.loop(0, 6)
    def _(step):
        core_copy(step).wait_send()
        drain(dfar_v.at[step], dnear_v.at[step], dgot_v.at[step], dtwo_v.at[step], d_sem.at[step])

    for i in range(nl // 2):

        @pl.when(core * (nl // 2) + i != me)
        def _():
            pltpu.make_async_remote_copy(
                zsend_v.at[i], zrecv_v.at[my_z], zsend_sem.at[i], zrecv_sem.at[my_z],
                device_id={"leaf": sibling}, device_id_type=MESH,
            ).wait_send()


def hand_on(conv_ref, head_ref, conv_out, head_out):
    conv_out[...] = conv_ref[...]
    head_out[...] = head_ref[...]


def body(audio, weight, head_weight, clip_owner, node_ids, *, nd, nl):
    nx = math.isqrt(nd)
    ny = nd // nx
    clips, length, chan = audio.shape
    nodes = head_weight.shape[0]
    routes = clip_owner.shape[1]
    pairs = node_ids.shape[2]
    cap = 2 * clips * routes // nl
    slots = nl * cap
    half = chan // 2
    rows_dp, cols_leaf = chan // nd, chan // nl
    span = nodes // nd
    filled = -(-6 * rows_dp // 128) * 128
    chunk = 48
    steps = clips // chunk
    a = jnp.transpose(audio, (1, 0, 2)).reshape(length // 3, 3, clips, chan)
    w = weight.reshape(2, 3 * chan, chan)
    own = jnp.transpose(clip_owner, (1, 0))
    ids = jnp.transpose(node_ids, (1, 2, 0))
    vm = pltpu.VMEM
    dma = pltpu.SemaphoreType.DMA
    scratch = [
        vm((9, 3, clips, chan), BF16),
        vm((2, 3 * chan, chan), BF16),
        vm((nodes, chan), BF16),
        vm((chan, nodes), BF16),
        vm((9, chunk, chan), F32),
        vm((9, chunk, chan), F32),
        vm((9, clips, chan), BF16),
        vm((9, clips, chan), F32),
        vm((3, clips, chan), F32),
        vm((clips, chan), BF16),
        vm((slots, clips), BF16),
        vm((nl, 2 * pairs, 128), BF16),
        vm((nl, 2 * pairs, 128), BF16),
        vm((slots, chan), BF16),
        vm((slots, chan), BF16),
        vm((slots, nodes), BF16),
        vm((slots, nodes), BF16),
        vm((slots, nodes), BF16),
        vm((slots, chan), BF16),
        vm((slots, chan), BF16),
        vm((ny, nx, span, chan), BF16),
        *[vm((2, 2, ny, span // 2, chan // 2), BF16) for _ in range(4)],
        vm((2, ny, span // 2, chan), BF16),
        vm((2, ny - 1, span // 2, chan), BF16),
        vm((3, clips, chan), BF16),
        vm((9, clips, chan), BF16),
        vm((6, chan, half), F32),
        vm((6, chan, half), BF16),
        vm((6, chan, half), BF16),
        vm((6, ny, nx, rows_dp, half), BF16),
        *[vm((6, 2, 2, ny, rows_dp // 2, half // 2), BF16) for _ in range(4)],
        vm((6, 2, ny, rows_dp // 2, half), BF16),
        vm((6, 2, ny - 1, rows_dp // 2, half), BF16),
        vm((filled, half), F32),
        vm((nl // 2, cols_leaf, filled), BF16),
        vm((nl // 2, cols_leaf, filled), BF16),
        vm((max(128, cols_leaf), filled), F32),
        dma((3,)), dma((steps,)), dma((2,)), dma((1,)), dma((nl,)), dma((2,)), dma((8, 2)),
        dma((6,)), dma((6,)), dma((6, 8, 2)), dma((nl // 2,)), dma((nl // 2,)),
    ]
    whole = pl.BlockSpec(memory_space=pltpu.VMEM)
    far = pl.BlockSpec(memory_space=pl.ANY)
    conv, head = pl.pallas_call(
        functools.partial(kernel, ny, nx, nl, chunk),
        out_shape=(
            jax.ShapeDtypeStruct((2, 3, rows_dp, cols_leaf), BF16),
            jax.ShapeDtypeStruct((nodes // nd, chan), BF16),
        ),
        in_specs=[far, far, far, whole, whole],
        out_specs=(whole, whole),
        scratch_shapes=scratch,
        compiler_params=pltpu.CompilerParams(
            collective_id=0, has_side_effects=True, vmem_limit_bytes=62914560
        ),
    )(a, w, head_weight, own, ids)
    return pl.pallas_call(
        hand_on,
        out_shape=(
            jax.ShapeDtypeStruct(conv.shape, BF16),
            jax.ShapeDtypeStruct(head.shape, BF16),
        ),
        in_specs=[whole, whole],
        out_specs=(whole, whole),
    )(conv, head)


def solution(mesh):
    placed = (
        P(("dp", "leaf"), None, None),
        P(),
        P("leaf", None),
        P(("dp", "leaf"), None),
        P(("dp", "leaf"), None, None),
    )
    return jax.shard_map(
        functools.partial(body, nd=mesh.shape["dp"], nl=mesh.shape["leaf"]),
        mesh=mesh,
        in_specs=placed,
        out_specs=(P(None, None, "dp", "leaf"), P(("leaf", "dp"), None)),
        check_vma=False,
    )
```

```python
import functools
import math

import jax
import jax.numpy as jnp
from jax import lax
from jax.experimental import pallas as pl
from jax.experimental.pallas import tpu as pltpu
from jax.sharding import PartitionSpec as P

MESH = pl.DeviceIdType.MESH
F32 = jnp.float32
BF16 = jnp.bfloat16
INV_ROOT_TWO = 0.7071067811865476
INV_ROOT_TWO_PI = 0.3989422804014327

NT = (((1,), (1,)), ((), ()))
TN = (((0,), (0,)), ((), ()))


def dot(a, b, dims=(((1,), (0,)), ((), ()))):
    return lax.dot_general(a, b, dims, preferred_element_type=F32)


def gelu_pair(value):
    half = 0.5 * (1.0 + lax.erf(value * INV_ROOT_TWO))
    bell = jnp.exp(-0.5 * value * value) * INV_ROOT_TWO_PI
    return value * half, half + value * bell


def bytes_wait(ref, sem):
    pltpu.make_async_copy(ref, ref, sem).wait()


def kernel(
    ny, nx, nl, chunk,
    a_hbm, w_hbm, h_hbm, own_ref, node_ref,
    conv_ref, head_ref,
    a_v, w_v, h_v, ht_v, pa_v, pb_v, a1_v, sl0_v, sl1_v, emb_v, d_v,
    nsend_v, nrecv_v, esend_v, erecv_v, call_v, cpos_v, st_v, gsend_v, grecv_v,
    hsend_v, hone_v, hmid_v, htwo_v, u1_v, u0_v, wown_v, wsend_v, wrecv_v,
    dsend_v, done_v, dmid_v, dtwo_v,
    g_v, zsend_v, zrecv_v, zsum_v,
    load_sem, a_sem, n_sem, e_sem, erecv_sem, g_sem, h_sem, csend_sem, crecv_sem,
    d_sem, zsend_sem, zrecv_sem,
):
    me = lax.axis_index("leaf")
    mine = lax.axis_index("dp")
    core = lax.rem(me, 2)
    sibling = me + 1 - 2 * core
    clips = emb_v.shape[0]
    chan = emb_v.shape[1]
    cap = esend_v.shape[0] // nl
    slots = nl * cap
    nodes = h_v.shape[0]
    pairs = node_ref.shape[1]
    nd = ny * nx
    my_y, my_x = mine // nx, lax.rem(mine, nx)
    half = chan // 2
    span = nodes // nd
    rows_dp = chan // nd
    cols_leaf = chan // nl
    steps = clips // chunk

    load_w0 = pltpu.make_async_copy(w_hbm.at[0], w_v.at[0], load_sem.at[0])
    load_w1 = pltpu.make_async_copy(w_hbm.at[1], w_v.at[1], load_sem.at[1])
    load_h = pltpu.make_async_copy(h_hbm, h_v, load_sem.at[2])

    def load_a(i):
        part = pl.ds(pl.multiple_of(i * chunk, chunk), chunk)
        return pltpu.make_async_copy(a_hbm.at[:, :, part], a_v.at[:, :, part], a_sem.at[i])

    load_w0.start()
    for i in range(steps):
        load_a(i).start()
    load_w1.start()
    load_h.start()

    barrier = pltpu.get_barrier_semaphore()

    @pl.loop(1, nl)
    def _(i):
        pl.semaphore_signal(
            barrier, inc=1, device_id={"leaf": lax.rem(me + i, nl)}, device_id_type=MESH
        )

    @pl.loop(1, nd)
    def _(i):
        pl.semaphore_signal(
            barrier, inc=1, device_id={"dp": lax.rem(mine + i, nd)}, device_id_type=MESH
        )

    owner_iota = lax.broadcasted_iota(jnp.int32, (nl, clips), 0)
    before = (
        lax.broadcasted_iota(jnp.int32, (clips, clips), 0)
        < lax.broadcasted_iota(jnp.int32, (clips, clips), 1)
    ).astype(F32).astype(BF16)
    slot_iota = lax.broadcasted_iota(jnp.int32, (slots, clips), 0)
    base = jnp.zeros((nl, 1), F32)
    spots = []
    lists = jnp.zeros((2 * pairs, slots), F32)
    for r in range(2):
        hit = (own_ref[r : r + 1, :] == owner_iota).astype(F32)
        rank = dot(hit.astype(BF16), before) + base
        base = base + jnp.sum(hit, axis=1, keepdims=True)

        place = jnp.sum(hit * (rank + (owner_iota * cap).astype(F32)), axis=0, keepdims=True)
        spots.append((slot_iota == place.astype(jnp.int32)).astype(F32).astype(BF16))
        ident = node_ref[r] + 1
        parts = jnp.concatenate([ident >> 7, ident & 127], axis=0).astype(F32).astype(BF16)
        lists = lists + dot(parts, spots[r], NT)
    d_v[...] = spots[0] + spots[1]
    blank = jnp.zeros((2 * pairs, 128 - cap), F32)
    for o in range(nl):
        listed = jnp.concatenate([lists[:, o * cap : (o + 1) * cap], blank], axis=1)
        nsend_v[o] = listed.astype(BF16)

    def block(i):
        return pl.ds(pl.multiple_of(i * cap, cap), cap)

    nz = nl // 2
    my_z = me // 2
    order = []
    for d in range(nz // 2 - 1, 0, -1):
        order.append((d, nz - d))
    order.insert(min(1, len(order)), (nz // 2, 0))
    order = [rel for pair in order for rel in pair]
    per = 4

    def leaf_at(rel, c):
        return 2 * lax.rem(my_z + rel, nz) + c

    def turn(rel):
        return order.index(rel % nz)

    def away():
        for rel in order:
            for c in range(2) if rel else (1 - core,):
                yield leaf_at(rel, c), 2 * turn(rel) + c, 2 * turn(-rel) + core

    home = 2 * turn(0) + core

    load_w0.wait()

    stage = [pa_v, pb_v]

    def multiply(i):
        load_a(i).wait()
        part = pl.ds(i * chunk, chunk)
        folded = jnp.concatenate(
            [a_v[:, k, part, :].reshape(9 * chunk, chan) for k in range(3)], axis=1
        )
        stage[i % 2][...] = dot(folded, w_v[0]).reshape(9, chunk, chan)

    def activate(i):
        part = pl.ds(i * chunk, chunk)

        @pl.loop(0, 9, unroll=True)
        def _(j):
            act, slope = gelu_pair(stage[i % 2][j])
            a1_v[j, part, :] = act.astype(BF16)
            sl0_v[j, part, :] = slope

    multiply(0)
    for i in range(steps):
        if i + 1 < steps:
            multiply(i + 1)
        activate(i)

    load_w1.wait()

    for side in range(2):
        cols = pl.ds(side * half, half)
        for j in range(3):
            folded = jnp.concatenate([a1_v[3 * j + k] for k in range(3)], axis=1)
            sl1_v[j, :, cols] = dot(folded, w_v[1, :, cols])

        @pl.loop(0, steps, unroll=True)
        def _(i):
            part = pl.ds(pl.multiple_of(i * chunk, chunk), chunk)
            total = jnp.zeros((chunk, half), F32)
            for j in range(3):
                act, slope = gelu_pair(sl1_v[j, part, cols])
                sl1_v[j, part, cols] = slope
                total = total + act
            emb_v[part, cols] = (total * (1.0 / 3.0)).astype(BF16)

        esend_v[:, cols] = dot(d_v[...], emb_v[:, cols]).astype(BF16)
        if side == 0:
            pl.semaphore_wait(barrier, nl - 1 + nd - 1)
            nrecv_v[home] = nsend_v[me]
            for to, _, mark in away():
                pltpu.make_async_remote_copy(
                    nsend_v.at[to], nrecv_v.at[mark], n_sem.at[0], n_sem.at[1],
                    device_id={"leaf": to}, device_id_type=MESH,
                ).start()
        for to, _, mark in away():
            pltpu.make_async_remote_copy(
                esend_v.at[block(to), cols], erecv_v.at[block(mark), cols], e_sem.at[0],
                erecv_sem.at[mark], device_id={"leaf": to}, device_id_type=MESH,
            ).start()
    erecv_v[block(home), :] = esend_v[block(me), :]

    load_h.wait()
    piece = nodes // 4

    for i in range(4):
        ht_v[:, i * piece : (i + 1) * piece] = h_v[i * piece : (i + 1) * piece, :].T

    bytes_wait(nsend_v.at[pl.ds(0, nl - 1)], n_sem.at[0])
    bytes_wait(nrecv_v.at[pl.ds(0, nl - 1)], n_sem.at[1])
    node_iota = lax.broadcasted_iota(jnp.int32, (16, nodes), 1).astype(F32)

    @pl.loop(0, nl)
    def _(o):
        parts = nrecv_v[o].astype(F32)
        named = (parts[:pairs] * 128.0 + parts[pairs:] - 1.0).T
        for i in range(cap // 16):
            part = pl.ds(pl.multiple_of(o * cap + i * 16, 16), 16)
            tally = jnp.zeros((16, nodes), F32)
            for q in range(pairs):
                weight = 17.0 if q < pairs // 2 else 1.0
                ident = named[i * 16 : (i + 1) * 16, q : q + 1]
                tally = tally + jnp.where(ident == node_iota, weight, 0.0)
            positive = jnp.floor(tally * (1.0 / 16.0))
            every = 0.5 * tally - 8.0 * positive
            call_v[part, :] = every.astype(BF16)
            cpos_v[part, :] = (every - positive).astype(BF16)

    lanes = nodes // 4
    for t in range(nl // per):
        sources = []
        for rel in order[2 * t : 2 * t + 2]:
            for c in range(2) if rel else (1 - core,):
                sources.append((leaf_at(rel, c), 2 * turn(rel) + c))
        for _, place in sources:
            bytes_wait(erecv_v.at[block(place)], erecv_sem.at[place])
        rows = pl.ds(t * per * cap, per * cap)
        emb = erecv_v[rows, :]

        for n in range(4):
            cols = pl.ds(n * lanes, lanes)
            score = dot(emb, ht_v[:, cols])
            st_v[rows, cols] = (
                jnp.tanh(0.5 * score) * call_v[rows, cols].astype(F32)
                + cpos_v[rows, cols].astype(F32)
            ).astype(BF16)

        gsend_v[rows, :] = dot(st_v[rows, :], h_v[...]).astype(BF16)
        if 0 in order[2 * t : 2 * t + 2]:
            grecv_v[block(me), :] = gsend_v[block(home), :]
        for to, place in sources:
            pltpu.make_async_remote_copy(
                gsend_v.at[block(place)], grecv_v.at[block(me)], g_sem.at[0], g_sem.at[1],
                device_id={"leaf": to}, device_id_type=MESH,
            ).start()

    low_rows, high_rows = pl.ds(0, span // 2), pl.ds(span // 2, span // 2)

    def over_x(o):
        return {"dp": my_y * nx + lax.rem(my_x + o, nx)}

    def over_y(o):
        return {"dp": lax.rem(my_y + o, ny) * nx + my_x}

    def send(source, target, sems, device):
        pltpu.make_async_remote_copy(
            source, target, sems.at[0], sems.at[1], device_id=device, device_id_type=MESH
        ).start()

    for o in range(1, ny + 1):
        y = lax.rem(my_y + o, ny)
        cols = pl.ds(pl.multiple_of(y * nx * span, nx * span), nx * span)
        terms = dot(st_v[:, cols], erecv_v[...], TN).astype(BF16)
        hsend_v[y] = terms.reshape(nx, span, chan)
        if o < ny:
            send(hsend_v.at[y, :, high_rows], hone_v.at[1, o - 1], h_sem.at[1], over_y(o))
    for o in range(1, nx):
        x = lax.rem(my_x + o, nx)
        send(hsend_v.at[:, x, low_rows], hone_v.at[0, o - 1], h_sem.at[0], over_x(o))

    strip = 32

    def head_middle():
        bytes_wait(hone_v.at[1], h_sem.at[1, 1])
        bytes_wait(hone_v.at[0], h_sem.at[0, 1])
        @pl.loop(0, ny)
        def _(i):
            for at in range(0, span // 2, strip):
                part = pl.ds(at, strip)
                total = hsend_v[i, my_x, part, :].astype(F32)
                for o in range(nx - 1):
                    total = total + hone_v[0, o, i, part, :].astype(F32)
                hmid_v[0, i, part, :] = total.astype(BF16)
                total = hsend_v[my_y, i, pl.ds(span // 2 + at, strip), :].astype(F32)
                for o in range(ny - 1):
                    total = total + hone_v[1, o, i, part, :].astype(F32)
                hmid_v[1, i, part, :] = total.astype(BF16)

        for o in range(1, ny):
            send(hmid_v.at[0, lax.rem(my_y + o, ny)], htwo_v.at[0, o - 1], h_sem.at[2], over_y(o))
            send(hmid_v.at[1, lax.rem(my_x + o, nx)], htwo_v.at[1, o - 1], h_sem.at[3], over_x(o))

    bytes_wait(grecv_v.at[pl.ds(0, (nl - 1) * cap)], g_sem.at[1])
    clip_grad = dot(d_v[...], grecv_v[...], TN) * (1.0 / 3.0)
    for j in range(3):
        u1_v[j] = (clip_grad * sl1_v[j]).astype(BF16)

    def leave(step, grad):
        low, high = grad[:, :half], grad[:, half:]
        wown_v[step] = jnp.where(core == 0, low, high)
        wsend_v[step] = jnp.where(core == 0, high, low).astype(BF16)
        core_copy(step).start()

    def core_copy(step):
        return pltpu.make_async_remote_copy(
            wsend_v.at[step], wrecv_v.at[step], csend_sem.at[step], crecv_sem.at[step],
            device_id={"leaf": sibling}, device_id_type=MESH,
        )

    part_rows = rows_dp // 2
    low_part, high_part = pl.ds(0, part_rows), pl.ds(part_rows, part_rows)

    def far_first(n):
        return sorted(range(1, n), key=lambda o: -min(o, n - o))

    def spread(step):
        core_copy(step).wait_recv()
        both = (wown_v[step] + wrecv_v[step].astype(F32)).astype(BF16)
        dsend_v[step] = both.reshape(ny, nx, rows_dp, half)
        for o in far_first(nx):
            x = lax.rem(my_x + o, nx)
            send(
                dsend_v.at[step, :, x, low_part], done_v.at[step, 0, o - 1],
                d_sem.at[step, 0], over_x(o),
            )
        for o in far_first(ny):
            y = lax.rem(my_y + o, ny)
            send(
                dsend_v.at[step, y, :, high_part], done_v.at[step, 1, o - 1],
                d_sem.at[step, 1], over_y(o),
            )

    def respread(step):
        bytes_wait(done_v.at[step, 0], d_sem.at[step, 0, 1])
        total = dsend_v[step, :, my_x, low_part, :].astype(F32)
        for o in range(nx - 1):
            total = total + done_v[step, 0, o].astype(F32)
        dmid_v[step, 0] = total.astype(BF16)
        bytes_wait(done_v.at[step, 1], d_sem.at[step, 1, 1])
        total = dsend_v[step, my_y, :, high_part, :].astype(F32)
        for o in range(ny - 1):
            total = total + done_v[step, 1, o].astype(F32)
        dmid_v[step, 1] = total.astype(BF16)
        for o in range(1, ny):
            send(
                dmid_v.at[step, 0, lax.rem(my_y + o, ny)], dtwo_v.at[step, 0, o - 1],
                d_sem.at[step, 2], over_y(o),
            )
            send(
                dmid_v.at[step, 1, lax.rem(my_x + o, nx)], dtwo_v.at[step, 1, o - 1],
                d_sem.at[step, 3], over_x(o),
            )

    def gather_step(step):
        for side, place in ((0, my_y), (1, my_x)):
            bytes_wait(dtwo_v.at[step, side], d_sem.at[step, 2 + side, 1])
            total = dmid_v[step, side, place].astype(F32)
            for o in range(ny - 1):
                total = total + dtwo_v[step, side, o].astype(F32)
            g_v[pl.ds(step * rows_dp + side * part_rows, part_rows), :] = total

    for k in range(3):
        left = jnp.concatenate([a1_v[3 * j + k] for j in range(3)], axis=0)
        leave(3 + k, dot(left, u1_v[...].reshape(3 * clips, chan), TN))

    for k in range(3):
        taps = w_v[1, k * chan : (k + 1) * chan, :]
        for j in range(3):
            u0_v[3 * j + k] = (dot(u1_v[j], taps, NT) * sl0_v[3 * j + k]).astype(BF16)
        spread(3 + k)

    for k in range(3):
        left = a_v[:, k].reshape(9 * clips, chan)
        leave(k, dot(left, u0_v[...].reshape(9 * clips, chan), TN))
        if k == 0:
            head_middle()
        else:
            spread(k - 1)

    spread(2)

    filled = 6 * rows_dp
    if g_v.shape[0] > filled:
        g_v[filled:, :] = jnp.zeros((g_v.shape[0] - filled, half), F32)

    for step in (3, 4, 5, 0, 1, 2):
        respread(step)

    for step in (3, 4, 5, 0, 1, 2):
        gather_step(step)

    zsend_v[...] = g_v[...].T.astype(BF16).reshape(nl // 2, cols_leaf, g_v.shape[0])
    for i in range(nl // 2):
        to = core * (nl // 2) + i

        @pl.when(to == me)
        def _():
            zrecv_v[my_z] = zsend_v[i]

        @pl.when(to != me)
        def _():
            pltpu.make_async_remote_copy(
                zsend_v.at[i], zrecv_v.at[my_z], zsend_sem.at[i], zrecv_sem.at[my_z],
                device_id={"leaf": to}, device_id_type=MESH,
            ).start()

    for side, place in ((0, my_y), (1, my_x)):
        bytes_wait(htwo_v.at[side], h_sem.at[2 + side, 1])
        for at in range(0, span // 2, strip):
            part = pl.ds(at, strip)
            total = hmid_v[side, place, part, :].astype(F32)
            for o in range(ny - 1):
                total = total + htwo_v[side, o, part, :].astype(F32)
            head_ref[pl.ds(side * (span // 2) + at, strip), :] = total.astype(BF16)

    giver = me // (nl // 2)
    zsum_v[...] = jnp.zeros(zsum_v.shape, F32)
    for z in range(nl // 2):

        @pl.when(2 * z + giver != me)
        def _():
            pltpu.make_async_remote_copy(
                zsend_v.at[z], zrecv_v.at[z], zsend_sem.at[z], zrecv_sem.at[z],
                device_id={"leaf": sibling}, device_id_type=MESH,
            ).wait_recv()

    total = zrecv_v[0].astype(F32)
    for z in range(1, nl // 2):
        total = total + zrecv_v[z].astype(F32)
    zsum_v[0:cols_leaf, :] = total
    final = zsum_v[...].T[:filled, :cols_leaf]
    conv_ref[...] = final.reshape(2, 3, rows_dp, cols_leaf).astype(BF16)

    bytes_wait(esend_v.at[pl.ds(0, (nl - 1) * cap)], e_sem.at[0])
    bytes_wait(gsend_v.at[pl.ds(0, (nl - 1) * cap)], g_sem.at[0])
    for side in range(2):
        bytes_wait(hone_v.at[side], h_sem.at[side, 0])
        bytes_wait(htwo_v.at[side], h_sem.at[2 + side, 0])

    @pl.loop(0, 6)
    def _(step):
        core_copy(step).wait_send()
        for side in range(2):
            bytes_wait(done_v.at[step, side], d_sem.at[step, side, 0])
            bytes_wait(dtwo_v.at[step, side], d_sem.at[step, 2 + side, 0])

    for i in range(nl // 2):

        @pl.when(core * (nl // 2) + i != me)
        def _():
            pltpu.make_async_remote_copy(
                zsend_v.at[i], zrecv_v.at[my_z], zsend_sem.at[i], zrecv_sem.at[my_z],
                device_id={"leaf": sibling}, device_id_type=MESH,
            ).wait_send()


def hand_on(conv_ref, head_ref, conv_out, head_out):
    conv_out[...] = conv_ref[...]
    head_out[...] = head_ref[...]


def body(audio, weight, head_weight, clip_owner, node_ids, *, nd, nl):
    nx = math.isqrt(nd)
    ny = nd // nx
    clips, length, chan = audio.shape
    nodes = head_weight.shape[0]
    routes = clip_owner.shape[1]
    pairs = node_ids.shape[2]
    cap = 2 * clips * routes // nl
    slots = nl * cap
    half = chan // 2
    rows_dp, cols_leaf = chan // nd, chan // nl
    span = nodes // nd
    filled = -(-6 * rows_dp // 128) * 128
    chunk = 48
    steps = clips // chunk
    a = jnp.transpose(audio, (1, 0, 2)).reshape(length // 3, 3, clips, chan)
    w = weight.reshape(2, 3 * chan, chan)
    own = jnp.transpose(clip_owner, (1, 0))
    ids = jnp.transpose(node_ids, (1, 2, 0))
    vm = pltpu.VMEM
    dma = pltpu.SemaphoreType.DMA
    scratch = [
        vm((9, 3, clips, chan), BF16),
        vm((2, 3 * chan, chan), BF16),
        vm((nodes, chan), BF16),
        vm((chan, nodes), BF16),
        vm((9, chunk, chan), F32),
        vm((9, chunk, chan), F32),
        vm((9, clips, chan), BF16),
        vm((9, clips, chan), F32),
        vm((3, clips, chan), F32),
        vm((clips, chan), BF16),
        vm((slots, clips), BF16),
        vm((nl, 2 * pairs, 128), BF16),
        vm((nl, 2 * pairs, 128), BF16),
        vm((slots, chan), BF16),
        vm((slots, chan), BF16),
        vm((slots, nodes), BF16),
        vm((slots, nodes), BF16),
        vm((slots, nodes), BF16),
        vm((slots, chan), BF16),
        vm((slots, chan), BF16),
        vm((ny, nx, span, chan), BF16),
        vm((2, ny - 1, ny, span // 2, chan), BF16),
        vm((2, ny, span // 2, chan), BF16),
        vm((2, ny - 1, span // 2, chan), BF16),
        vm((3, clips, chan), BF16),
        vm((9, clips, chan), BF16),
        vm((6, chan, half), F32),
        vm((6, chan, half), BF16),
        vm((6, chan, half), BF16),
        vm((6, ny, nx, rows_dp, half), BF16),
        vm((6, 2, ny - 1, ny, rows_dp // 2, half), BF16),
        vm((6, 2, ny, rows_dp // 2, half), BF16),
        vm((6, 2, ny - 1, rows_dp // 2, half), BF16),
        vm((filled, half), F32),
        vm((nl // 2, cols_leaf, filled), BF16),
        vm((nl // 2, cols_leaf, filled), BF16),
        vm((max(128, cols_leaf), filled), F32),
        dma((3,)), dma((steps,)), dma((2,)), dma((1,)), dma((nl,)), dma((2,)), dma((4, 2)),
        dma((6,)), dma((6,)), dma((6, 4, 2)), dma((nl // 2,)), dma((nl // 2,)),
    ]
    whole = pl.BlockSpec(memory_space=pltpu.VMEM)
    far = pl.BlockSpec(memory_space=pl.ANY)
    conv, head = pl.pallas_call(
        functools.partial(kernel, ny, nx, nl, chunk),
        out_shape=(
            jax.ShapeDtypeStruct((2, 3, rows_dp, cols_leaf), BF16),
            jax.ShapeDtypeStruct((nodes // nd, chan), BF16),
        ),
        in_specs=[far, far, far, whole, whole],
        out_specs=(whole, whole),
        scratch_shapes=scratch,
        compiler_params=pltpu.CompilerParams(
            collective_id=0, has_side_effects=True, vmem_limit_bytes=62914560
        ),
    )(a, w, head_weight, own, ids)
    return pl.pallas_call(
        hand_on,
        out_shape=(
            jax.ShapeDtypeStruct(conv.shape, BF16),
            jax.ShapeDtypeStruct(head.shape, BF16),
        ),
        in_specs=[whole, whole],
        out_specs=(whole, whole),
    )(conv, head)


def solution(mesh):
    placed = (
        P(("dp", "leaf"), None, None),
        P(),
        P("leaf", None),
        P(("dp", "leaf"), None),
        P(("dp", "leaf"), None, None),
    )
    return jax.shard_map(
        functools.partial(body, nd=mesh.shape["dp"], nl=mesh.shape["leaf"]),
        mesh=mesh,
        in_specs=placed,
        out_specs=(P(None, None, "dp", "leaf"), P(("leaf", "dp"), None)),
        check_vma=False,
    )
```

```python
import functools
import math

import jax
import jax.numpy as jnp
from jax import lax
from jax.experimental import pallas as pl
from jax.experimental.pallas import tpu as pltpu
from jax.sharding import PartitionSpec as P

MESH = pl.DeviceIdType.MESH
F32 = jnp.float32
BF16 = jnp.bfloat16
INV_ROOT_TWO = 0.7071067811865476
INV_ROOT_TWO_PI = 0.3989422804014327

NT = (((1,), (1,)), ((), ()))
TN = (((0,), (0,)), ((), ()))


def dot(a, b, dims=(((1,), (0,)), ((), ()))):
    return lax.dot_general(a, b, dims, preferred_element_type=F32)


def gelu_pair(value):
    half = 0.5 * (1.0 + lax.erf(value * INV_ROOT_TWO))
    bell = jnp.exp(-0.5 * value * value) * INV_ROOT_TWO_PI
    return value * half, half + value * bell


def bytes_wait(ref, sem):
    pltpu.make_async_copy(ref, ref, sem).wait()


def kernel(
    ny, nx, nl, chunk,
    a_hbm, w_hbm, h_hbm, own_ref, node_ref,
    conv_ref, head_ref,
    a_v, w_v, h_v, ht_v, pa_v, pb_v, a1_v, sl0_v, sl1_v, emb_v, d_v,
    nsend_v, nrecv_v, esend_v, erecv_v, call_v, cpos_v, st_v, gsend_v, grecv_v,
    hsend_v, hone_v, hmid_v, htwo_v, u1_v, u0_v, wown_v, wsend_v, wrecv_v,
    dsend_v, done_v, dmid_v, dtwo_v,
    g_v, zsend_v, zrecv_v, zsum_v,
    load_sem, a_sem, n_sem, e_sem, erecv_sem, g_sem, h_sem, csend_sem, crecv_sem,
    d_sem, zsend_sem, zrecv_sem,
):
    me = lax.axis_index("leaf")
    mine = lax.axis_index("dp")
    core = lax.rem(me, 2)
    sibling = me + 1 - 2 * core
    clips = emb_v.shape[0]
    chan = emb_v.shape[1]
    cap = esend_v.shape[0] // nl
    slots = nl * cap
    nodes = h_v.shape[0]
    pairs = node_ref.shape[1]
    nd = ny * nx
    my_y, my_x = mine // nx, lax.rem(mine, nx)
    half = chan // 2
    span = nodes // nd
    rows_dp = chan // nd
    cols_leaf = chan // nl
    steps = clips // chunk

    load_w0 = pltpu.make_async_copy(w_hbm.at[0], w_v.at[0], load_sem.at[0])
    load_w1 = pltpu.make_async_copy(w_hbm.at[1], w_v.at[1], load_sem.at[1])
    load_h = pltpu.make_async_copy(h_hbm, h_v, load_sem.at[2])

    def load_a(i):
        part = pl.ds(pl.multiple_of(i * chunk, chunk), chunk)
        return pltpu.make_async_copy(a_hbm.at[:, :, part], a_v.at[:, :, part], a_sem.at[i])

    load_w0.start()
    for i in range(steps):
        load_a(i).start()
    load_w1.start()
    load_h.start()

    barrier = pltpu.get_barrier_semaphore()

    @pl.loop(1, nl)
    def _(i):
        pl.semaphore_signal(
            barrier, inc=1, device_id={"leaf": lax.rem(me + i, nl)}, device_id_type=MESH
        )

    @pl.loop(1, nd)
    def _(i):
        pl.semaphore_signal(
            barrier, inc=1, device_id={"dp": lax.rem(mine + i, nd)}, device_id_type=MESH
        )

    owner_iota = lax.broadcasted_iota(jnp.int32, (nl, clips), 0)
    before = (
        lax.broadcasted_iota(jnp.int32, (clips, clips), 0)
        < lax.broadcasted_iota(jnp.int32, (clips, clips), 1)
    ).astype(F32).astype(BF16)
    slot_iota = lax.broadcasted_iota(jnp.int32, (slots, clips), 0)
    base = jnp.zeros((nl, 1), F32)
    spots = []
    lists = jnp.zeros((2 * pairs, slots), F32)
    for r in range(2):
        hit = (own_ref[r : r + 1, :] == owner_iota).astype(F32)
        rank = dot(hit.astype(BF16), before) + base
        base = base + jnp.sum(hit, axis=1, keepdims=True)

        place = jnp.sum(hit * (rank + (owner_iota * cap).astype(F32)), axis=0, keepdims=True)
        spots.append((slot_iota == place.astype(jnp.int32)).astype(F32).astype(BF16))
        ident = node_ref[r] + 1
        parts = jnp.concatenate([ident >> 7, ident & 127], axis=0).astype(F32).astype(BF16)
        lists = lists + dot(parts, spots[r], NT)
    d_v[...] = spots[0] + spots[1]
    blank = jnp.zeros((2 * pairs, 128 - cap), F32)
    for o in range(nl):
        listed = jnp.concatenate([lists[:, o * cap : (o + 1) * cap], blank], axis=1)
        nsend_v[o] = listed.astype(BF16)

    def block(i):
        return pl.ds(pl.multiple_of(i * cap, cap), cap)

    nz = nl // 2
    my_z = me // 2
    order = []
    for d in range(nz // 2 - 1, 0, -1):
        order.append((d, nz - d))
    order.insert(min(1, len(order)), (nz // 2, 0))
    order = [rel for pair in order for rel in pair]
    per = 4

    def leaf_at(rel, c):
        return 2 * lax.rem(my_z + rel, nz) + c

    def turn(rel):
        return order.index(rel % nz)

    def away():
        for rel in order:
            for c in range(2) if rel else (1 - core,):
                yield leaf_at(rel, c), 2 * turn(rel) + c, 2 * turn(-rel) + core

    home = 2 * turn(0) + core

    load_w0.wait()

    stage = [pa_v, pb_v]

    def multiply(i):
        load_a(i).wait()
        part = pl.ds(i * chunk, chunk)
        folded = jnp.concatenate(
            [a_v[:, k, part, :].reshape(9 * chunk, chan) for k in range(3)], axis=1
        )
        stage[i % 2][...] = dot(folded, w_v[0]).reshape(9, chunk, chan)

    def activate(i):
        part = pl.ds(i * chunk, chunk)

        @pl.loop(0, 9, unroll=True)
        def _(j):
            act, slope = gelu_pair(stage[i % 2][j])
            a1_v[j, part, :] = act.astype(BF16)
            sl0_v[j, part, :] = slope

    multiply(0)
    for i in range(steps):
        if i + 1 < steps:
            multiply(i + 1)
        activate(i)

    load_w1.wait()

    for side in range(2):
        cols = pl.ds(side * half, half)
        for j in range(3):
            folded = jnp.concatenate([a1_v[3 * j + k] for k in range(3)], axis=1)
            sl1_v[j, :, cols] = dot(folded, w_v[1, :, cols])

        @pl.loop(0, steps, unroll=True)
        def _(i):
            part = pl.ds(pl.multiple_of(i * chunk, chunk), chunk)
            total = jnp.zeros((chunk, half), F32)
            for j in range(3):
                act, slope = gelu_pair(sl1_v[j, part, cols])
                sl1_v[j, part, cols] = slope
                total = total + act
            emb_v[part, cols] = (total * (1.0 / 3.0)).astype(BF16)

        esend_v[:, cols] = dot(d_v[...], emb_v[:, cols]).astype(BF16)
        if side == 0:
            pl.semaphore_wait(barrier, nl - 1 + nd - 1)
            nrecv_v[home] = nsend_v[me]
            for to, _, mark in away():
                pltpu.make_async_remote_copy(
                    nsend_v.at[to], nrecv_v.at[mark], n_sem.at[0], n_sem.at[1],
                    device_id={"leaf": to}, device_id_type=MESH,
                ).start()
        for to, _, mark in away():
            pltpu.make_async_remote_copy(
                esend_v.at[block(to), cols], erecv_v.at[block(mark), cols], e_sem.at[0],
                erecv_sem.at[mark], device_id={"leaf": to}, device_id_type=MESH,
            ).start()
    erecv_v[block(home), :] = esend_v[block(me), :]

    load_h.wait()
    piece = nodes // 4

    for i in range(4):
        ht_v[:, i * piece : (i + 1) * piece] = h_v[i * piece : (i + 1) * piece, :].T

    bytes_wait(nsend_v.at[pl.ds(0, nl - 1)], n_sem.at[0])
    bytes_wait(nrecv_v.at[pl.ds(0, nl - 1)], n_sem.at[1])
    node_iota = lax.broadcasted_iota(jnp.int32, (16, nodes), 1).astype(F32)

    @pl.loop(0, nl)
    def _(o):
        parts = nrecv_v[o].astype(F32)
        named = (parts[:pairs] * 128.0 + parts[pairs:] - 1.0).T
        for i in range(cap // 16):
            part = pl.ds(pl.multiple_of(o * cap + i * 16, 16), 16)
            tally = jnp.zeros((16, nodes), F32)
            for q in range(pairs):
                weight = 17.0 if q < pairs // 2 else 1.0
                ident = named[i * 16 : (i + 1) * 16, q : q + 1]
                tally = tally + jnp.where(ident == node_iota, weight, 0.0)
            positive = jnp.floor(tally * (1.0 / 16.0))
            every = 0.5 * tally - 8.0 * positive
            call_v[part, :] = every.astype(BF16)
            cpos_v[part, :] = (every - positive).astype(BF16)

    lanes = nodes // 4
    for t in range(nl // per):
        sources = []
        for rel in order[2 * t : 2 * t + 2]:
            for c in range(2) if rel else (1 - core,):
                sources.append((leaf_at(rel, c), 2 * turn(rel) + c))
        for _, place in sources:
            bytes_wait(erecv_v.at[block(place)], erecv_sem.at[place])
        rows = pl.ds(t * per * cap, per * cap)
        emb = erecv_v[rows, :]

        for n in range(4):
            cols = pl.ds(n * lanes, lanes)
            score = dot(emb, ht_v[:, cols])
            st_v[rows, cols] = (
                jnp.tanh(0.5 * score) * call_v[rows, cols].astype(F32)
                + cpos_v[rows, cols].astype(F32)
            ).astype(BF16)

        gsend_v[rows, :] = dot(st_v[rows, :], h_v[...]).astype(BF16)
        if 0 in order[2 * t : 2 * t + 2]:
            grecv_v[block(me), :] = gsend_v[block(home), :]
        for to, place in sources:
            pltpu.make_async_remote_copy(
                gsend_v.at[block(place)], grecv_v.at[block(me)], g_sem.at[0], g_sem.at[1],
                device_id={"leaf": to}, device_id_type=MESH,
            ).start()

    low_rows, high_rows = pl.ds(0, span // 2), pl.ds(span // 2, span // 2)

    def over_x(o):
        return {"dp": my_y * nx + lax.rem(my_x + o, nx)}

    def over_y(o):
        return {"dp": lax.rem(my_y + o, ny) * nx + my_x}

    def send(source, target, sems, device):
        pltpu.make_async_remote_copy(
            source, target, sems.at[0], sems.at[1], device_id=device, device_id_type=MESH
        ).start()

    for o in range(1, ny + 1):
        y = lax.rem(my_y + o, ny)
        cols = pl.ds(pl.multiple_of(y * nx * span, nx * span), nx * span)
        terms = dot(st_v[:, cols], erecv_v[...], TN).astype(BF16)
        hsend_v[y] = terms.reshape(nx, span, chan)
        if o < ny:
            send(hsend_v.at[y, :, high_rows], hone_v.at[1, o - 1], h_sem.at[1], over_y(o))
    for o in range(1, nx):
        x = lax.rem(my_x + o, nx)
        send(hsend_v.at[:, x, low_rows], hone_v.at[0, o - 1], h_sem.at[0], over_x(o))

    strip = 32

    def head_middle():
        bytes_wait(hone_v.at[1], h_sem.at[1, 1])
        bytes_wait(hone_v.at[0], h_sem.at[0, 1])
        @pl.loop(0, ny)
        def _(i):
            for at in range(0, span // 2, strip):
                part = pl.ds(at, strip)
                total = hsend_v[i, my_x, part, :].astype(F32)
                for o in range(nx - 1):
                    total = total + hone_v[0, o, i, part, :].astype(F32)
                hmid_v[0, i, part, :] = total.astype(BF16)
                total = hsend_v[my_y, i, pl.ds(span // 2 + at, strip), :].astype(F32)
                for o in range(ny - 1):
                    total = total + hone_v[1, o, i, part, :].astype(F32)
                hmid_v[1, i, part, :] = total.astype(BF16)

        for o in range(1, ny):
            send(hmid_v.at[0, lax.rem(my_y + o, ny)], htwo_v.at[0, o - 1], h_sem.at[2], over_y(o))
            send(hmid_v.at[1, lax.rem(my_x + o, nx)], htwo_v.at[1, o - 1], h_sem.at[3], over_x(o))

    bytes_wait(grecv_v.at[pl.ds(0, (nl - 1) * cap)], g_sem.at[1])
    clip_grad = dot(d_v[...], grecv_v[...], TN) * (1.0 / 3.0)
    for j in range(3):
        u1_v[j] = (clip_grad * sl1_v[j]).astype(BF16)

    def leave(step, grad):
        low, high = grad[:, :half], grad[:, half:]
        wown_v[step] = jnp.where(core == 0, low, high)
        wsend_v[step] = jnp.where(core == 0, high, low).astype(BF16)
        core_copy(step).start()

    def core_copy(step):
        return pltpu.make_async_remote_copy(
            wsend_v.at[step], wrecv_v.at[step], csend_sem.at[step], crecv_sem.at[step],
            device_id={"leaf": sibling}, device_id_type=MESH,
        )

    part_rows = rows_dp // 2
    low_part, high_part = pl.ds(0, part_rows), pl.ds(part_rows, part_rows)

    def far_first(n):
        return sorted(range(1, n), key=lambda o: -min(o, n - o))

    def spread(step):
        core_copy(step).wait_recv()
        both = (wown_v[step] + wrecv_v[step].astype(F32)).astype(BF16)
        dsend_v[step] = both.reshape(ny, nx, rows_dp, half)
        for o in far_first(nx):
            x = lax.rem(my_x + o, nx)
            send(
                dsend_v.at[step, :, x, low_part], done_v.at[step, 0, o - 1],
                d_sem.at[step, 0], over_x(o),
            )
        for o in far_first(ny):
            y = lax.rem(my_y + o, ny)
            send(
                dsend_v.at[step, y, :, high_part], done_v.at[step, 1, o - 1],
                d_sem.at[step, 1], over_y(o),
            )

    def respread(step):
        bytes_wait(done_v.at[step, 0], d_sem.at[step, 0, 1])
        total = dsend_v[step, :, my_x, low_part, :].astype(F32)
        for o in range(nx - 1):
            total = total + done_v[step, 0, o].astype(F32)
        dmid_v[step, 0] = total.astype(BF16)
        bytes_wait(done_v.at[step, 1], d_sem.at[step, 1, 1])
        total = dsend_v[step, my_y, :, high_part, :].astype(F32)
        for o in range(ny - 1):
            total = total + done_v[step, 1, o].astype(F32)
        dmid_v[step, 1] = total.astype(BF16)
        for o in range(1, ny):
            send(
                dmid_v.at[step, 0, lax.rem(my_y + o, ny)], dtwo_v.at[step, 0, o - 1],
                d_sem.at[step, 2], over_y(o),
            )
            send(
                dmid_v.at[step, 1, lax.rem(my_x + o, nx)], dtwo_v.at[step, 1, o - 1],
                d_sem.at[step, 3], over_x(o),
            )

    def gather_step(step):
        for side, place in ((0, my_y), (1, my_x)):
            bytes_wait(dtwo_v.at[step, side], d_sem.at[step, 2 + side, 1])
            total = dmid_v[step, side, place].astype(F32)
            for o in range(ny - 1):
                total = total + dtwo_v[step, side, o].astype(F32)
            g_v[pl.ds(step * rows_dp + side * part_rows, part_rows), :] = total

    for k in range(3):
        left = jnp.concatenate([a1_v[3 * j + k] for j in range(3)], axis=0)
        leave(3 + k, dot(left, u1_v[...].reshape(3 * clips, chan), TN))

    for k in range(3):
        taps = w_v[1, k * chan : (k + 1) * chan, :]
        for j in range(3):
            u0_v[3 * j + k] = (dot(u1_v[j], taps, NT) * sl0_v[3 * j + k]).astype(BF16)
        spread(3 + k)

    for k in range(3):
        left = a_v[:, k].reshape(9 * clips, chan)
        leave(k, dot(left, u0_v[...].reshape(9 * clips, chan), TN))
        if k > 0:
            spread(k - 1)

    spread(2)
    head_middle()

    filled = 6 * rows_dp
    if g_v.shape[0] > filled:
        g_v[filled:, :] = jnp.zeros((g_v.shape[0] - filled, half), F32)

    for step in (3, 4, 5, 0, 1, 2):
        respread(step)

    for step in (3, 4, 5, 0, 1, 2):
        gather_step(step)

    zsend_v[...] = g_v[...].T.astype(BF16).reshape(nl // 2, cols_leaf, g_v.shape[0])
    for i in range(nl // 2):
        to = core * (nl // 2) + i

        @pl.when(to == me)
        def _():
            zrecv_v[my_z] = zsend_v[i]

        @pl.when(to != me)
        def _():
            pltpu.make_async_remote_copy(
                zsend_v.at[i], zrecv_v.at[my_z], zsend_sem.at[i], zrecv_sem.at[my_z],
                device_id={"leaf": to}, device_id_type=MESH,
            ).start()

    for side, place in ((0, my_y), (1, my_x)):
        bytes_wait(htwo_v.at[side], h_sem.at[2 + side, 1])
        for at in range(0, span // 2, strip):
            part = pl.ds(at, strip)
            total = hmid_v[side, place, part, :].astype(F32)
            for o in range(ny - 1):
                total = total + htwo_v[side, o, part, :].astype(F32)
            head_ref[pl.ds(side * (span // 2) + at, strip), :] = total.astype(BF16)

    giver = me // (nl // 2)
    zsum_v[...] = jnp.zeros(zsum_v.shape, F32)
    for z in range(nl // 2):

        @pl.when(2 * z + giver != me)
        def _():
            pltpu.make_async_remote_copy(
                zsend_v.at[z], zrecv_v.at[z], zsend_sem.at[z], zrecv_sem.at[z],
                device_id={"leaf": sibling}, device_id_type=MESH,
            ).wait_recv()

    total = zrecv_v[0].astype(F32)
    for z in range(1, nl // 2):
        total = total + zrecv_v[z].astype(F32)
    zsum_v[0:cols_leaf, :] = total
    final = zsum_v[...].T[:filled, :cols_leaf]
    conv_ref[...] = final.reshape(2, 3, rows_dp, cols_leaf).astype(BF16)

    bytes_wait(esend_v.at[pl.ds(0, (nl - 1) * cap)], e_sem.at[0])
    bytes_wait(gsend_v.at[pl.ds(0, (nl - 1) * cap)], g_sem.at[0])
    for side in range(2):
        bytes_wait(hone_v.at[side], h_sem.at[side, 0])
        bytes_wait(htwo_v.at[side], h_sem.at[2 + side, 0])

    @pl.loop(0, 6)
    def _(step):
        core_copy(step).wait_send()
        for side in range(2):
            bytes_wait(done_v.at[step, side], d_sem.at[step, side, 0])
            bytes_wait(dtwo_v.at[step, side], d_sem.at[step, 2 + side, 0])

    for i in range(nl // 2):

        @pl.when(core * (nl // 2) + i != me)
        def _():
            pltpu.make_async_remote_copy(
                zsend_v.at[i], zrecv_v.at[my_z], zsend_sem.at[i], zrecv_sem.at[my_z],
                device_id={"leaf": sibling}, device_id_type=MESH,
            ).wait_send()


def hand_on(conv_ref, head_ref, conv_out, head_out):
    conv_out[...] = conv_ref[...]
    head_out[...] = head_ref[...]


def body(audio, weight, head_weight, clip_owner, node_ids, *, nd, nl):
    nx = math.isqrt(nd)
    ny = nd // nx
    clips, length, chan = audio.shape
    nodes = head_weight.shape[0]
    routes = clip_owner.shape[1]
    pairs = node_ids.shape[2]
    cap = 2 * clips * routes // nl
    slots = nl * cap
    half = chan // 2
    rows_dp, cols_leaf = chan // nd, chan // nl
    span = nodes // nd
    filled = -(-6 * rows_dp // 128) * 128
    chunk = 48
    steps = clips // chunk
    a = jnp.transpose(audio, (1, 0, 2)).reshape(length // 3, 3, clips, chan)
    w = weight.reshape(2, 3 * chan, chan)
    own = jnp.transpose(clip_owner, (1, 0))
    ids = jnp.transpose(node_ids, (1, 2, 0))
    vm = pltpu.VMEM
    dma = pltpu.SemaphoreType.DMA
    scratch = [
        vm((9, 3, clips, chan), BF16),
        vm((2, 3 * chan, chan), BF16),
        vm((nodes, chan), BF16),
        vm((chan, nodes), BF16),
        vm((9, chunk, chan), F32),
        vm((9, chunk, chan), F32),
        vm((9, clips, chan), BF16),
        vm((9, clips, chan), F32),
        vm((3, clips, chan), F32),
        vm((clips, chan), BF16),
        vm((slots, clips), BF16),
        vm((nl, 2 * pairs, 128), BF16),
        vm((nl, 2 * pairs, 128), BF16),
        vm((slots, chan), BF16),
        vm((slots, chan), BF16),
        vm((slots, nodes), BF16),
        vm((slots, nodes), BF16),
        vm((slots, nodes), BF16),
        vm((slots, chan), BF16),
        vm((slots, chan), BF16),
        vm((ny, nx, span, chan), BF16),
        vm((2, ny - 1, ny, span // 2, chan), BF16),
        vm((2, ny, span // 2, chan), BF16),
        vm((2, ny - 1, span // 2, chan), BF16),
        vm((3, clips, chan), BF16),
        vm((9, clips, chan), BF16),
        vm((6, chan, half), F32),
        vm((6, chan, half), BF16),
        vm((6, chan, half), BF16),
        vm((6, ny, nx, rows_dp, half), BF16),
        vm((6, 2, ny - 1, ny, rows_dp // 2, half), BF16),
        vm((6, 2, ny, rows_dp // 2, half), BF16),
        vm((6, 2, ny - 1, rows_dp // 2, half), BF16),
        vm((filled, half), F32),
        vm((nl // 2, cols_leaf, filled), BF16),
        vm((nl // 2, cols_leaf, filled), BF16),
        vm((max(128, cols_leaf), filled), F32),
        dma((3,)), dma((steps,)), dma((2,)), dma((1,)), dma((nl,)), dma((2,)), dma((4, 2)),
        dma((6,)), dma((6,)), dma((6, 4, 2)), dma((nl // 2,)), dma((nl // 2,)),
    ]
    whole = pl.BlockSpec(memory_space=pltpu.VMEM)
    far = pl.BlockSpec(memory_space=pl.ANY)
    conv, head = pl.pallas_call(
        functools.partial(kernel, ny, nx, nl, chunk),
        out_shape=(
            jax.ShapeDtypeStruct((2, 3, rows_dp, cols_leaf), BF16),
            jax.ShapeDtypeStruct((nodes // nd, chan), BF16),
        ),
        in_specs=[far, far, far, whole, whole],
        out_specs=(whole, whole),
        scratch_shapes=scratch,
        compiler_params=pltpu.CompilerParams(
            collective_id=0, has_side_effects=True, vmem_limit_bytes=62914560
        ),
    )(a, w, head_weight, own, ids)
    return pl.pallas_call(
        hand_on,
        out_shape=(
            jax.ShapeDtypeStruct(conv.shape, BF16),
            jax.ShapeDtypeStruct(head.shape, BF16),
        ),
        in_specs=[whole, whole],
        out_specs=(whole, whole),
    )(conv, head)


def solution(mesh):
    placed = (
        P(("dp", "leaf"), None, None),
        P(),
        P("leaf", None),
        P(("dp", "leaf"), None),
        P(("dp", "leaf"), None, None),
    )
    return jax.shard_map(
        functools.partial(body, nd=mesh.shape["dp"], nl=mesh.shape["leaf"]),
        mesh=mesh,
        in_specs=placed,
        out_specs=(P(None, None, "dp", "leaf"), P(("leaf", "dp"), None)),
        check_vma=False,
    )
```
